256 devices in a mesh: attn: 8 (over z_hi, core), ffn: 8 (over z_lo, x), tp: 4 (over y).
Axes of the slice: x: 4, y: 4, z: 8 (z_hi: 4, z_lo: 2; z = z_hi * 2 + z_lo), core: 2. Of those that a mesh axis runs over, the one named last changes fastest.
Arguments:
- queries: bfloat16 [2048, 4096], P(('attn', 'ffn'), 'tp'), may hold values from -4.5 to 4.5
- keys: bfloat16 [2048, 128, 512], P(('attn', 'ffn'), None, 'tp'), may hold values from -4.5 to 4.5
- values: bfloat16 [2048, 128, 512], P(('attn', 'ffn'), None, 'tp'), may hold values from -4.5 to 4.5
- lengths: int32 [2048], P(('attn', 'ffn')), may hold values from 0 to 128, as said below
- routes: int32 [2048, 1], P(('attn', 'ffn')), may hold values from 0 to 7; in each aligned block of 32 rows (0 to 31, 32 to 63, ...) at most 8 rows name the same one
- residual: bfloat16 [2048, 4096], P(('attn', 'ffn')), may hold values from -20 to 20
- w_out: bfloat16 [4096, 4096], P(None, ('attn', 'tp')), may hold values from -0.09375 to 0.09375
- norm_gain: float32 [4096], P(('attn', 'tp')), may hold values from 0.1 to 1.9
- w_gate: bfloat16 [8, 4096, 14336], P('ffn', None, ('attn', 'tp')), may hold values from -0.09375 to 0.09375
- w_up: bfloat16 [8, 4096, 14336], P('ffn', None, ('attn', 'tp')), may hold values from -0.09375 to 0.09375
- w_down: bfloat16 [8, 14336, 4096], P('ffn', ('attn', 'tp')), may hold values from -0.09375 to 0.09375
Outputs:
- stream: bfloat16 [2048, 4096], P(('attn', 'ffn'))
- group_sums: float32 [8, 4096], P('ffn', ('attn', 'tp'))
The draws below stay inside these ranges and needn't reach their ends.
Inputs may be any that keep to these rules, and one draw needn't show every extreme that they name: `lengths`: 0 marks an empty slot, else the number of cached positions of its candidate. `routes`: in each aligned block of 32 rows no group is named by more than 8 rows.
All inputs are finite; a program needn't handle non-finite values.
Results may differ from the reference program's by a relative error of at most 0.018.
Values may be sent and summed in bfloat16 or wider, within the bound.
A program may use at most 128 MiB of HBM per device.

```python
import math
import jax
import jax.numpy as jnp
import numpy as np
from jax import lax

D = 4096
FF = 14336
QH = 32
KVH = 4
HD = 128
LEN = 128
SLOTS = 32
CAP = 8
ALL = 2048
N_FFN = 8


def draw_queries(key, part):
    key = jax.random.fold_in(key, 11)
    shape = (ALL, KVH, QH // KVH, HD)
    base = jnp.clip(jax.random.normal(key, shape, jnp.float32), -4.5, 4.5)
    return base.reshape(ALL, QH * HD).astype(jnp.bfloat16)


def draw_keys(key, part):
    key = jax.random.fold_in(key, 13)
    shape = (ALL, LEN, KVH, HD)
    base = jnp.clip(jax.random.normal(key, shape, jnp.float32), -4.5, 4.5)
    return base.reshape(ALL, LEN, KVH * HD).astype(jnp.bfloat16)


def draw_residual(key, part):
    key = jax.random.fold_in(key, 17)
    base_key, row_key, col_key = jax.random.split(key, 3)
    row_scale = jnp.exp(jax.random.uniform(row_key, (ALL, 1), jnp.float32, math.log(0.3), math.log(3.0)))
    ramp = jnp.exp(lax.broadcasted_iota(jnp.float32, (1, D), 1) * (math.log(3.0) / D))
    col_scale = jnp.exp(jax.random.uniform(col_key, (1, D), jnp.float32, math.log(0.5), math.log(1.5))) * ramp
    base = jnp.clip(jax.random.normal(base_key, (ALL, D), jnp.float32), -4.0, 4.0)
    return jnp.clip(base * row_scale * col_scale, -20.0, 20.0).astype(jnp.bfloat16)


def draw_lengths(key, part):
    key = jax.random.fold_in(key, 19)
    count_key, size_key, full_key = jax.random.split(key, 3)
    column_count = ALL // SLOTS
    counts = jax.random.randint(count_key, (column_count,), max(1, SLOTS // 4), SLOTS + 1)
    full_column = jax.random.randint(full_key, (), 0, column_count)
    counts = jnp.where(jnp.arange(column_count) == full_column, SLOTS, counts)
    index = jnp.arange(ALL)
    occupied = index % SLOTS < counts[index // SLOTS]
    sizes = jax.random.randint(size_key, (ALL,), 1, LEN + 1)
    sizes = jnp.where(index == full_column * SLOTS, LEN, sizes)
    return jnp.where(occupied, sizes, 0).astype(jnp.int32)


def strengthened(drawn, stream_key, source, target, shards_of, factor):
    def block_of(dim):
        return (jnp.arange(drawn.shape[dim]) // (drawn.shape[dim] // shards_of)).reshape((-1,) + (1,) * (drawn.ndim - 1 - dim))

    first = jax.random.permutation(stream_key, shards_of)[block_of(target)]
    other_side = (block_of(target) + shards_of // 2) % shards_of
    return jnp.where((block_of(source) == first) | (block_of(source) == other_side), factor * drawn, drawn)


def level_of(stream_key, shape, cuts, smallest, largest):
    def one(dim, shards_of):
        draws = jax.random.uniform(jax.random.fold_in(jax.random.fold_in(stream_key, 6), dim), (shards_of,), jnp.float32, smallest / len(cuts), largest / len(cuts))
        return jnp.repeat(jnp.exp(draws), shape[dim] // shards_of).reshape((-1,) + (1,) * (len(shape) - dim - 1))

    gain = one(*cuts[0])
    for cut in cuts[1:]:
        gain = gain * one(*cut)
    return gain


def routed_block(own_key, own, number, rows, amount, top, bound, lean):
    sequence = jax.random.permutation(own_key, amount)
    packed, common = shares(amount, rows * top, bound, lean, True), shares(amount, rows * top, bound, lean, False)
    places = jnp.arange(amount)

    def named(tallies, turn):
        used = int((tallies > 0).sum())
        fixed = max(1, used // 4)
        moved = fixed + (places - fixed + turn * (used - fixed)) % max(1, amount - fixed)
        return jnp.zeros((amount,), jnp.int32).at[sequence[jnp.where(places < fixed, places, moved)]].set(jnp.asarray(tallies, jnp.int32))

    tallies = jnp.where(number % 4 == 0, named(packed, number // 4), named(common, number - number // 4 - 1))
    mixed = jax.random.permutation(jax.random.fold_in(own, 3), amount)
    giver, receiver = mixed[0:amount // 2 * 2:2], mixed[1:amount // 2 * 2:2]
    margin = jnp.minimum(tallies[giver] - 1, bound - tallies[receiver]) // 2
    margin = jnp.where((giver == sequence[0]) | (receiver == sequence[0]) | (tallies[receiver] == 0), 0, jnp.maximum(margin, 0))
    moved = jax.random.randint(jax.random.fold_in(own, 4), (amount // 2,), 0, 1 << 20) % (margin + 1)
    tallies = tallies.at[giver].add(-moved).at[receiver].add(moved)
    members = jnp.searchsorted(jnp.cumsum(tallies), jnp.arange(rows * top), side="right").astype(jnp.int32)
    table = members.reshape(top, rows).T
    table = table[jax.random.permutation(jax.random.fold_in(own, 1), rows)]
    turn = jax.random.randint(jax.random.fold_in(own, 2), (rows, 1), 0, top)
    return jnp.take_along_axis(table, (jnp.arange(top)[None, :] + turn) % top, axis=1)


def shares(number_of, total, limit, skew, full):
    weights = [(1 << 20) // math.isqrt(grade ** skew) + 1 for grade in range(1, number_of + 1)]
    largest = limit if full else min(limit, max(-(-total // number_of), total * weights[0] // sum(weights)))
    least = 1 if total - largest >= number_of - 1 else 0
    given, rest = [largest] + [least] * (number_of - 1), total - largest - least * (number_of - 1)
    while rest > 0:
        candidates = [i for i in range(1, number_of) if given[i] < largest] or [i for i in range(1, number_of) if given[i] < limit]
        whole, budget = sum([weights[i] for i in candidates]), rest
        for i in candidates:
            extra = min(limit - given[i], max(1, budget * weights[i] // whole), rest)
            given[i] = given[i] + extra
            rest = rest - extra
    return np.array(given)


def scatter_about(stream_key, shape, width, bound, pieces=(), kind=jnp.bfloat16):
    loudness = level_of(stream_key, shape, pieces, -0.22, 0.18) if pieces else 1.0
    array = jax.random.normal(stream_key, shape, jnp.float32) * width * loudness
    return jnp.minimum(jnp.maximum(array, -bound), bound).astype(kind)


def gaussian_with(own_key, shape, width, limit, cuts, heavy, kind=jnp.bfloat16):
    drawn = width * jax.random.normal(own_key, shape, jnp.float32)
    if cuts:
        drawn = drawn * level_of(own_key, shape, cuts, -0.22, 0.18)
    return jnp.clip(strengthened(drawn, jax.random.fold_in(own_key, 3), *heavy), -limit, limit).astype(kind)


def setup_inputs(seed: int = 0) -> dict:
    splits = jax.random.split(jax.random.key(seed), 12)
    queries = draw_queries(jax.random.fold_in(splits[11], 71), 0)
    keys = draw_keys(jax.random.fold_in(splits[11], 71), 0)
    values = scatter_about(splits[2], (ALL, LEN, KVH * HD), 1.0, 4.5, ((0, 64), (2, 4)))
    lengths = draw_lengths(jax.random.fold_in(splits[11], 71), 0)
    routes_keys = jax.random.split(jax.random.fold_in(splits[4], 1), ALL // SLOTS)
    routes_turns = jax.random.permutation(jax.random.fold_in(splits[4], 3), ALL // SLOTS)
    routes = jax.vmap(lambda own, number: routed_block(jax.random.fold_in(splits[4], 2), own, number, SLOTS, N_FFN, 1, CAP, 1))(routes_keys, routes_turns).reshape((ALL, 1))
    residual = draw_residual(jax.random.fold_in(splits[11], 71), 0)
    w_out = scatter_about(splits[6], (QH * HD, D), (QH * HD) ** -0.5, 0.09375, ((1, 32),))
    norm_gain = jnp.clip(1.0 + 0.18 * jax.random.normal(splits[7], (D,), jnp.float32), 0.1, 1.9)
    w_gate = scatter_about(splits[8], (N_FFN, D, FF), D ** -0.5, 0.09375, ((0, 8), (2, 32)))
    w_up = scatter_about(splits[9], (N_FFN, D, FF), D ** -0.5, 0.09375, ((0, 8), (2, 32)))
    w_down = gaussian_with(splits[10], (N_FFN, FF, D), FF ** -0.5, 0.09375, ((0, 8), (1, 32)), (1, 2, 32, 2.75))
    return {"queries": queries, "keys": keys, "values": values, "lengths": lengths, "routes": routes, "residual": residual, "w_out": w_out, "norm_gain": norm_gain, "w_gate": w_gate, "w_up": w_up, "w_down": w_down}


EPSILON = 1e-05

def reference(queries, keys, values, lengths, routes, residual, w_out, norm_gain, w_gate, w_up, w_down):
    row_count = queries.shape[0]
    group_size = QH // KVH
    query_heads = queries.astype(jnp.float32).reshape(row_count, KVH, group_size, HD)
    key_heads = keys.astype(jnp.float32).reshape(row_count, LEN, KVH, HD)
    value_heads = values.astype(jnp.float32).reshape(row_count, LEN, KVH, HD)
    scores = jnp.einsum('skgd,slkd->skgl', query_heads, key_heads) / math.sqrt(HD)
    valid = lax.broadcasted_iota(jnp.int32, (row_count, LEN), 1) < lengths[:, None]
    valid_mask = valid[:, None, None, :]
    row_max = lax.optimization_barrier(jnp.max(jnp.where(valid_mask, scores, -1e+30), axis=-1, keepdims=True))
    unnormed = jnp.where(valid_mask, jnp.exp(scores - row_max), 0.0)
    summed = jnp.maximum(lax.optimization_barrier(jnp.sum(unnormed, axis=-1, keepdims=True)), 1.0)
    weights = (unnormed / summed).astype(jnp.bfloat16)
    combined = jnp.einsum('skgl,slkd->skgd', weights.astype(jnp.float32), value_heads)
    attended = combined.reshape(row_count, QH * HD).astype(jnp.bfloat16)
    hidden = residual.astype(jnp.float32) + jnp.dot(attended, w_out, preferred_element_type=jnp.float32)
    inverse_rms = lax.rsqrt(lax.optimization_barrier(jnp.sum(hidden * hidden, axis=1)) / D + EPSILON)
    normed = (hidden * inverse_rms[:, None] * norm_gain[None, :]).astype(jnp.bfloat16)
    occupied = lengths > 0
    destination = routes[:, 0]
    block_count = row_count // SLOTS
    dest_blocks = destination.reshape(block_count, SLOTS)
    occ_blocks = occupied.reshape(block_count, SLOTS)
    earlier = lax.broadcasted_iota(jnp.int32, (SLOTS, SLOTS), 1) < lax.broadcasted_iota(jnp.int32, (SLOTS, SLOTS), 0)
    same_group = (dest_blocks[:, :, None] == dest_blocks[:, None, :]) & occ_blocks[:, None, :] & earlier[None, :, :]
    rank_in_group = lax.optimization_barrier(jnp.sum(same_group.astype(jnp.int32), axis=2))
    normed_blocks = normed.astype(jnp.float32).reshape(block_count, SLOTS, D)
    slot_iota = lax.broadcasted_iota(jnp.int32, (block_count, CAP, SLOTS), 1)

    def one_group(group):
        chosen = (dest_blocks == group) & occ_blocks
        placing = ((slot_iota == rank_in_group[:, None, :]) & chosen[:, None, :]).astype(jnp.float32)
        gathered = jnp.einsum('bcs,bsd->bcd', placing, normed_blocks, precision=lax.Precision.HIGHEST)
        gathered = gathered.reshape(block_count * CAP, D).astype(jnp.bfloat16)
        gate_sum = jnp.dot(gathered, w_gate[group], preferred_element_type=jnp.float32)
        up_sum = jnp.dot(gathered, w_up[group], preferred_element_type=jnp.float32)
        activated = (jax.nn.silu(gate_sum) * up_sum).astype(jnp.bfloat16)
        down_rows = jnp.dot(activated, w_down[group], preferred_element_type=jnp.float32).reshape(block_count, CAP, D)
        return jnp.einsum('bcs,bcd->bsd', placing, down_rows, precision=lax.Precision.HIGHEST)

    def accumulate(total, group):
        return (total + one_group(group), None)
    start = jnp.zeros((block_count, SLOTS, D), jnp.float32)
    down_blocks, _ = lax.scan(accumulate, start, jnp.arange(N_FFN, dtype=jnp.int32))
    down_sum = down_blocks.reshape(row_count, D)
    stream = jnp.where(occupied[:, None], hidden + down_sum, 0.0).astype(jnp.bfloat16)
    choose = (destination[:, None] == lax.broadcasted_iota(jnp.int32, (row_count, N_FFN), 1)) & occupied[:, None]
    group_sums = jnp.dot(choose.astype(jnp.float32).T, down_sum, precision=lax.Precision.HIGHEST)
    return (stream, group_sums)
```

```python
import functools
import math

import jax
import jax.numpy as jnp
from jax import lax
from jax.experimental import pallas as pl
from jax.experimental.pallas import tpu as pltpu
from jax.sharding import PartitionSpec as P

HD = 128
EPSILON = 1e-05
MESH = pl.DeviceIdType.MESH
BF = jnp.bfloat16
F32 = jnp.float32
Z_ORDER = (1, 3, 2)
RS_ORDER = (2, 1, 3, 0)


def iota(shape, dim):
    return lax.broadcasted_iota(jnp.int32, shape, dim)


def position():
    return lax.axis_index("attn"), lax.axis_index("ffn"), lax.axis_index("tp")


def remote(src, dst, send, recv, device):
    return pltpu.make_async_remote_copy(
        src_ref=src, dst_ref=dst, send_sem=send, recv_sem=recv, device_id=device, device_id_type=MESH
    )


def greet(devices):
    barrier = pltpu.get_barrier_semaphore()
    for device in devices:
        pl.semaphore_signal(barrier, inc=1, device_id=device, device_id_type=MESH)
    return lambda: pl.semaphore_wait(barrier, len(devices))


def gather_group(buf, half, zs, zr, ys, yr, hs, hr, cs, cr, consume):
    a, f, t = position()
    right, left = lax.rem(t + 1, 4), lax.rem(t + 3, 4)
    opposite = lax.rem(t + 2, 4)
    sibling = a + 1 - 2 * lax.rem(a, 2)
    rows = buf.shape[2]
    first, second = pl.ds(0, half), pl.ds(half, rows - half)
    source = [a] + [lax.rem(a + 8 - 2 * dz, 8) for dz in Z_ORDER]
    sent = []

    def start(copy):
        copy.start()
        sent.append(copy)

    def z_send(k):
        start(remote(buf.at[a, t], buf.at[a, t], zs.at[k], zr.at[k], (lax.rem(a + 2 * Z_ORDER[k], 8), f, t)))

    def z_wait(k):
        slot = buf.at[source[k + 1], t]
        remote(slot, slot, zs.at[k], zr.at[k], (a, f, right)).wait_recv()

    def y_send(k):
        slot = buf.at[source[k], t]
        start(remote(slot, slot, ys.at[k, 0], yr.at[k, 0], (a, f, right)))
        start(remote(slot, slot, ys.at[k, 1], yr.at[k, 1], (a, f, left)))

    def y_forward(k):
        slot = buf.at[source[k], left]
        remote(slot, slot, ys.at[k, 0], yr.at[k, 0], (a, f, right)).wait_recv()
        piece = slot.at[first]
        start(remote(piece, piece, hs.at[k, 0], hr.at[k, 0], (a, f, right)))
        slot = buf.at[source[k], right]
        remote(slot, slot, ys.at[k, 1], yr.at[k, 1], (a, f, left)).wait_recv()
        piece = slot.at[second]
        start(remote(piece, piece, hs.at[k, 1], hr.at[k, 1], (a, f, left)))

    def core_send(k):
        slot = buf.at[source[k], opposite]
        remote(slot.at[first], slot.at[first], hs.at[k, 0], hr.at[k, 0], (a, f, right)).wait_recv()
        remote(slot.at[second], slot.at[second], hs.at[k, 1], hr.at[k, 1], (a, f, left)).wait_recv()
        chunk = buf.at[source[k]]
        start(remote(chunk, chunk, cs.at[k], cr.at[k], (sibling, f, t)))

    def core_wait(k):
        other = source[k] + 1 - 2 * lax.rem(a, 2)
        chunk = buf.at[other]
        remote(chunk, chunk, cs.at[k], cr.at[k], (sibling, f, t)).wait_recv()
        consume(lax.div(source[k], 2))

    for k in range(3):
        z_send(k)
    y_send(0)
    z_wait(0)
    y_send(1)
    y_forward(0)
    z_wait(1)
    y_send(2)
    y_forward(1)
    core_send(0)
    z_wait(2)
    y_send(3)
    y_forward(2)
    core_send(1)
    core_wait(0)
    y_forward(3)
    core_send(2)
    core_wait(1)
    core_send(3)
    core_wait(2)
    core_wait(3)
    return sent


GATHER_SEMS = [
    pltpu.SemaphoreType.DMA((3,)),
    pltpu.SemaphoreType.DMA((3,)),
    pltpu.SemaphoreType.DMA((4, 2)),
    pltpu.SemaphoreType.DMA((4, 2)),
    pltpu.SemaphoreType.DMA((4, 2)),
    pltpu.SemaphoreType.DMA((4, 2)),
    pltpu.SemaphoreType.DMA((4,)),
    pltpu.SemaphoreType.DMA((4,)),
]


def attend(q, k, v, lens, att):
    for part in range(2):
        base = part * 16
        heads = jnp.concatenate([q[base : base + 16, h * HD : (h + 1) * HD] for h in range(8)], axis=0)
        slot = lax.rem(iota((128, 128), 0), 16)
        scores = jnp.zeros((128, 128), F32)
        for pair in range(8):
            block = k[base + 2 * pair : base + 2 * pair + 2].reshape(256, HD)
            both = lax.dot_general(heads, block, (((1,), (1,)), ((), ())), preferred_element_type=F32)
            scores = jnp.where(slot == 2 * pair, both[:, :128], scores)
            scores = jnp.where(slot == 2 * pair + 1, both[:, 128:], scores)
        scores = scores / math.sqrt(HD)
        limit = jnp.concatenate([lens[base : base + 16, :]] * 8, axis=0)
        valid = iota((128, 128), 1) < limit
        top = jnp.max(jnp.where(valid, scores, -1e30), axis=-1, keepdims=True)
        unnormed = jnp.where(valid, jnp.exp(scores - top), 0.0)
        summed = jnp.maximum(jnp.sum(unnormed, axis=-1, keepdims=True), 1.0)
        weights = unnormed / summed
        total = jnp.zeros((128, HD), F32)
        for pair in range(8):
            block = v[base + 2 * pair : base + 2 * pair + 2].reshape(256, HD)
            masked = jnp.concatenate(
                [jnp.where(slot == 2 * pair, weights, 0.0), jnp.where(slot == 2 * pair + 1, weights, 0.0)], axis=1
            ).astype(BF)
            total = total + jnp.dot(masked, block, preferred_element_type=F32)
        total = total.astype(BF)
        for h in range(8):
            att[pl.ds(base, 16), pl.ds(h * HD, HD)] = total[h * 16 : (h + 1) * 16, :]


def project_kernel(
    q_hbm, k_hbm, v_hbm, lens, codes, res_hbm, wout_hbm,
    h_out, hidden, back_out, table_out, need_out,
    q, k, v, wout, buf, res, cbuf, place, sbuf, hbuf, tsend, tbuf,
    in_sems, rs, rr, es, er, fs, fr, gs, gr, own_sem, *gather_sems,
):
    a, f, t = position()
    loads = []
    for i, (src, dst) in enumerate(((q_hbm, q), (k_hbm, k), (v_hbm, v), (wout_hbm, wout))):
        copy = pltpu.make_async_copy(src, dst, in_sems.at[i])
        copy.start()
        loads.append(copy)
    attn_peers = [lax.rem(a + step, 8) for step in range(1, 8)]
    ffn_peers = [lax.rem(f + step, 8) for step in range(1, 8)]
    all_here = greet(
        [(peer, f, t) for peer in attn_peers]
        + [(a, peer, t) for peer in ffn_peers]
        + [(a, f, lax.rem(t + 1, 4)), (a, f, lax.rem(t + 3, 4))]
    )
    all_here()

    def columns(index):
        return pl.ds(pl.multiple_of((index * 4 + t) * HD, HD), HD)

    sent = []
    cbuf[a] = codes[...]
    for i, peer in enumerate(attn_peers):
        copy = remote(res_hbm.at[:, columns(peer)], res.at[a], rs.at[i], rr.at[i], (peer, f, t))
        copy.start()
        sent.append(copy)
        copy = remote(codes, cbuf.at[a], es.at[i], er.at[i], (peer, f, t))
        copy.start()
        sent.append(copy)
    own = pltpu.make_async_copy(res_hbm.at[:, columns(a)], res.at[a], own_sem)
    own.start()
    for copy in loads[:3]:
        copy.wait()
    attend(q, k, v, lens, buf.at[a, t])

    def consume(z):
        pair = pl.ds(2 * z, 2)
        total = jnp.zeros((64, HD), F32)
        for other in range(4):
            left = buf[pair, other].reshape(64, 1024)
            total = total + jnp.dot(left, wout[pl.ds(other * 1024, 1024), :], preferred_element_type=F32)
        total = total + res[pair].reshape(64, HD).astype(F32)
        hidden[pl.ds(pl.multiple_of(z * 64, 64), 64), :] = total

    def prepare():
        loads[3].wait()
        own.wait()
        for i in range(7):
            peer = lax.rem(a + 7 - i, 8)
            remote(res.at[peer], res.at[peer], rs.at[i], rr.at[i], (peer, f, t)).wait_recv()
            remote(cbuf.at[peer], cbuf.at[peer], es.at[i], er.at[i], (peer, f, t)).wait_recv()
        code = cbuf[0]
        for i in range(1, 8):
            code = code + cbuf[i]
        code = code - 1
        code_t = jnp.broadcast_to(code.astype(F32), (256, 256)).T.astype(jnp.int32)
        down, across = iota((256, 256), 0), iota((256, 256), 1)
        same = (code_t == code) & (down // 32 == across // 32)
        rank_row = jnp.sum(jnp.where(same & (down < across), 1.0, 0.0), axis=0, keepdims=True)
        rank_col = jnp.sum(jnp.where(same & (across < down), 1.0, 0.0), axis=1, keepdims=True)
        target_row = code * 8 + rank_row.astype(jnp.int32)
        target_col = code_t[:, 0:1] * 8 + rank_col.astype(jnp.int32)
        p, q_index = iota((512, 256), 0), iota((512, 256), 1)
        hit = ((p // 64) * 8 + lax.rem(p, 8) == target_row) & (lax.rem(p // 8, 8) == q_index // 32)
        place[...] = jnp.where(hit, 1.0, 0.0).astype(BF)
        q_index, p = iota((256, 512), 0), iota((256, 512), 1)
        hit = ((p // 64) * 8 + lax.rem(p, 8) == target_col) & (lax.rem(p // 8, 8) == q_index // 32)
        back_out[...] = jnp.where(hit, 1.0, 0.0).astype(BF)
        q_index, j = iota((256, 128), 0), iota((256, 128), 1)
        named = (code_t[:, :128] == j // 8) & (q_index // 32 == lax.rem(j, 8)) & (j < 64)
        tsend[...] = jnp.sum(jnp.where(named, 1.0, 0.0), axis=0, keepdims=True)
        tbuf[f] = tsend[...]

    first = [True]

    def prepared(z):
        if first[0]:
            prepare()
            for i, peer in enumerate(ffn_peers):
                copy = remote(tsend, tbuf.at[f], gs.at[i], gr.at[i], (a, peer, t))
                copy.start()
                sent.append(copy)
            first[0] = False
        consume(z)

    sent += gather_group(buf, 16, *gather_sems, prepared)
    routed = jnp.dot(place[...], hidden[...].astype(BF), preferred_element_type=F32).astype(BF)
    sbuf[...] = routed.reshape(8, 64, HD)
    for i, peer in enumerate(ffn_peers):
        copy = remote(sbuf.at[peer], hbuf.at[f], fs.at[i], fr.at[i], (a, peer, t))
        copy.start()
        sent.append(copy)
    hbuf[f] = sbuf[f]
    for i in range(7):
        peer = lax.rem(f + 7 - i, 8)
        remote(tbuf.at[peer], tbuf.at[peer], gs.at[i], gr.at[i], (a, peer, t)).wait_recv()
    table = tbuf[...].reshape(8, 128)
    table_out[...] = table
    sums = jnp.broadcast_to(jnp.sum(table, axis=0, keepdims=True), (16, 128)).astype(BF)
    fold = jnp.where(iota((128, 128), 0) // 8 == iota((128, 128), 1), 1.0, 0.0).astype(BF)
    totals = jnp.dot(sums, fold, preferred_element_type=F32)
    most = jnp.max(totals, axis=1, keepdims=True)[:8]
    need_out[...] = jnp.broadcast_to(most, (8, 128)).astype(jnp.int32)
    for i in range(7):
        peer = lax.rem(f + 7 - i, 8)
        remote(hbuf.at[peer], hbuf.at[peer], fs.at[i], fr.at[i], (a, peer, t)).wait_recv()
    h_out[...] = hbuf[...].reshape(512, HD)
    for copy in sent:
        copy.wait_send()


def ffn_kernel(
    rows,
    h_ref, hidden, back, table, gain, wg_hbm, wu_hbm, wd_hbm,
    stream_out, sums_out,
    wg, wu, wd, buf, gate, up, act, csend, crecv, part, y1s, y1r, y2s, y2r, zsend, zrecv, unplace, rsend, rbuf, final,
    line, in_sems, kcs, kcr, k1s, k1r, k2s, k2r, kzs, kzr, kbs, kbr, kas, kar, kys, kyr, *gather_sems,
):
    a, f, t = position()
    z, core = lax.div(a, 2), lax.rem(a, 2)
    right, left, opposite = lax.rem(t + 1, 4), lax.rem(t + 3, 4), lax.rem(t + 2, 4)
    sibling = a + 1 - 2 * core
    half = rows // 2
    blocks = rows // 128
    loads = []
    for i, (src, dst) in enumerate(((wg_hbm, wg), (wu_hbm, wu), (wd_hbm, wd))):
        copy = pltpu.make_async_copy(src, dst, in_sems.at[i])
        copy.start()
        loads.append(copy)
    attn_peers = [lax.rem(a + step, 8) for step in range(1, 8)]
    ffn_peers = [lax.rem(f + step, 8) for step in range(1, 8)]
    tp_peers = [lax.rem(t + step, 4) for step in range(1, 4)]

    all_here = greet(
        [(peer, f, t) for peer in attn_peers]
        + [(a, peer, t) for peer in ffn_peers]
        + [(a, f, peer) for peer in tp_peers]
    )

    j, p = iota((128, 512), 0), iota((128, 512), 1)
    pick = jnp.where(j == f * 8 + lax.rem(p // 8, 8), 1.0, 0.0).astype(BF)
    table16 = jnp.concatenate([table[...], table[...]], axis=0).astype(BF)
    counts = jnp.dot(table16, pick, preferred_element_type=F32)[:8]
    s, p = iota((8, 512), 0), iota((8, 512), 1)
    counts = jnp.sum(jnp.where(s == p // 64, counts, 0.0), axis=0, keepdims=True)
    live = lax.rem(iota((1, 512), 1), 8).astype(F32) < counts
    flags = jnp.broadcast_to(jnp.where(live, 1.0, 0.0), (16, 512)).astype(BF)
    before = jnp.where(iota((512, 512), 0) < iota((512, 512), 1), 1.0, 0.0).astype(BF)
    place = jnp.dot(flags, before, preferred_element_type=F32)[:1]
    place = jnp.where(live, place, -1.0).astype(jnp.int32)
    compact = jnp.where(iota((rows, 512), 0) == place, 1.0, 0.0).astype(BF)
    picked = jnp.dot(compact, h_ref[...], preferred_element_type=F32)
    slot = buf.at[a, t]
    slot[pl.ds(0, rows), :] = (picked * gain[...]).astype(BF)
    squares = picked * picked
    tail = jnp.zeros((16, 128), F32)
    line_index = iota((16, 128), 0)
    for i in range(blocks):
        block = jnp.sum(squares[i * 128 : (i + 1) * 128].T, axis=0, keepdims=True)
        high = block.astype(BF).astype(F32)
        tail = jnp.where(line_index == i, high, tail)
        tail = jnp.where(line_index == blocks + i, block - high, tail)
    slot[pl.ds(rows, 16), :] = tail.astype(BF)

    all_here()

    first = [True]

    def consume(chunk):
        if first[0]:
            loads[0].wait()
            loads[1].wait()
            place_t = jnp.broadcast_to(place.astype(F32), (128, 512)).T.astype(jnp.int32)
            for i in range(blocks):
                hit = place_t == iota((512, 128), 1) + i * 128
                unplace[:, pl.ds(i * 128, 128)] = jnp.where(hit, 1.0, 0.0).astype(BF)
        for c in range(2):
            index = chunk * 2 + c
            depth = pl.ds(pl.multiple_of(index * 512, 512), 512)
            for m in range(0, rows, 256):
                span = pl.ds(m, 256)
                lhs = jnp.concatenate([buf[index, other, span, :] for other in range(4)], axis=1)
                for weight, total in ((wg, gate), (wu, up)):
                    value = lax.dot_general(
                        lhs, weight[:, depth], (((1,), (1,)), ((), ())), preferred_element_type=F32
                    )
                    if first[0] and c == 0:
                        total[span, :] = value
                    else:
                        total[span, :] += value
        first[0] = False

    sent = gather_group(buf, half + 16, *gather_sems, consume)

    tails = jnp.sum(buf[:, :, pl.ds(rows, 16), :].astype(F32).reshape(32, 16, 128), axis=0)
    for i in range(blocks):
        span = pl.ds(i * 128, 128)
        total = tails[i : i + 1] + tails[blocks + i : blocks + i + 1]
        inverse = lax.rsqrt(total / 4096.0 + EPSILON)
        scale = jnp.broadcast_to(inverse, (128, 128)).T
        scale = jnp.concatenate([scale] * 4, axis=1)[:, :448]
        g = gate[span, :] * scale
        act[span, :] = (g / (1.0 + jnp.exp(-g)) * (up[span, :] * scale)).astype(BF)
    loads[2].wait()

    def start(copy):
        copy.start()
        sent.append(copy)

    def chunk_columns(dz, c):
        index = lax.rem(z + dz, 4) * 2 + c
        return pl.ds(pl.multiple_of(index * 512, 512), 512)

    def down(dz, c, store):
        for m in range(0, rows, 256):
            span = pl.ds(m, 256)
            store(span, jnp.dot(act[span, :], wd[:, chunk_columns(dz, c)], preferred_element_type=F32))

    def give(i):
        def store(span, value):
            csend[i, span, :] = value.astype(BF)

        down(RS_ORDER[i], 1 - core, store)
        start(remote(csend.at[i], crecv.at[i], kcs.at[i], kcr.at[i], (sibling, f, t)))

    def keep(i):
        def store(span, value):
            part[i, span, :] = value

        down(RS_ORDER[i], core, store)

    def lanes(index):
        return pl.ds(pl.multiple_of(index * HD, HD), HD)

    top, low = pl.ds(0, half), pl.ds(half, half)

    def y_first(i):
        remote(csend.at[i], crecv.at[i], kcs.at[i], kcr.at[i], (sibling, f, t)).wait_recv()
        part[i] += crecv[i].astype(F32)
        y1s[i, 0, top, :] = part[i, top, lanes(opposite)].astype(BF)
        y1s[i, 0, low, :] = part[i, low, lanes(right)].astype(BF)
        start(remote(y1s.at[i, 0], y1r.at[i, 0], k1s.at[i, 0], k1r.at[i, 0], (a, f, right)))
        y1s[i, 1, top, :] = part[i, top, lanes(left)].astype(BF)
        y1s[i, 1, low, :] = part[i, low, lanes(opposite)].astype(BF)
        start(remote(y1s.at[i, 1], y1r.at[i, 1], k1s.at[i, 1], k1r.at[i, 1], (a, f, left)))

    def y_second(i):
        remote(y1s.at[i, 0], y1r.at[i, 0], k1s.at[i, 0], k1r.at[i, 0], (a, f, right)).wait_recv()
        y2s[i, 0] = (part[i, top, lanes(right)] + y1r[i, 0, top, :].astype(F32)).astype(BF)
        start(remote(y2s.at[i, 0], y2r.at[i, 0], k2s.at[i, 0], k2r.at[i, 0], (a, f, right)))
        remote(y1s.at[i, 1], y1r.at[i, 1], k1s.at[i, 1], k1r.at[i, 1], (a, f, left)).wait_recv()
        y2s[i, 1] = (part[i, low, lanes(left)] + y1r[i, 1, low, :].astype(F32)).astype(BF)
        start(remote(y2s.at[i, 1], y2r.at[i, 1], k2s.at[i, 1], k2r.at[i, 1], (a, f, left)))

    def y_sum(i):
        remote(y2s.at[i, 0], y2r.at[i, 0], k2s.at[i, 0], k2r.at[i, 0], (a, f, right)).wait_recv()
        remote(y2s.at[i, 1], y2r.at[i, 1], k2s.at[i, 1], k2r.at[i, 1], (a, f, left)).wait_recv()
        upper = part[i, top, lanes(t)] + y1r[i, 1, top, :].astype(F32) + y2r[i, 0].astype(F32)
        lower = part[i, low, lanes(t)] + y1r[i, 0, low, :].astype(F32) + y2r[i, 1].astype(F32)
        return upper, lower

    def z_give(i):
        dz = RS_ORDER[i]
        upper, lower = y_sum(i)
        zsend[i, top, :] = upper.astype(BF)
        zsend[i, low, :] = lower.astype(BF)
        start(remote(zsend.at[i], zrecv.at[i], kzs.at[i], kzr.at[i], (lax.rem(a + 2 * dz, 8), f, t)))

    give(0)
    keep(0)
    give(1)
    keep(1)
    y_first(0)
    give(2)
    keep(2)
    y_first(1)
    give(3)
    y_second(0)
    keep(3)
    y_first(2)
    y_second(1)
    y_first(3)
    z_give(0)
    y_second(2)
    z_give(1)
    y_second(3)
    z_give(2)
    total = jnp.concatenate(y_sum(3), axis=0)
    for i in range(3):
        remote(zsend.at[i], zrecv.at[i], kzs.at[i], kzr.at[i], (sibling, f, t)).wait_recv()
        total = total + zrecv[i].astype(F32)

    sums_out[...] = jnp.sum(total, axis=0, keepdims=True)
    spread = jnp.dot(unplace[...], total.astype(BF), preferred_element_type=F32).astype(BF)
    rsend[...] = spread.reshape(8, 64, HD)
    for i, peer in enumerate(ffn_peers):
        start(remote(rsend.at[peer], rbuf.at[f], kbs.at[i], kbr.at[i], (a, peer, t)))
    rbuf[f] = rsend[f]
    live_rows = jnp.sum(back[...].astype(F32), axis=1, keepdims=True) > 0.5
    for i in range(7):
        peer = lax.rem(f + 7 - i, 8)
        remote(rbuf.at[peer], rbuf.at[peer], kbs.at[i], kbr.at[i], (a, peer, t)).wait_recv()
    returned = jnp.dot(back[...], rbuf[...].reshape(512, HD), preferred_element_type=F32)
    line[...] = jnp.where(live_rows, hidden[...] + returned, 0.0).astype(BF).reshape(8, 32, HD)
    for i, peer in enumerate(attn_peers):
        start(remote(line.at[peer], final.at[t, a], kas.at[i], kar.at[i], (peer, f, t)))
    final[t, a] = line[a]
    for i in range(7):
        peer = lax.rem(a + 7 - i, 8)
        remote(final.at[t, peer], final.at[t, peer], kas.at[i], kar.at[i], (peer, f, t)).wait_recv()
    for i, peer in enumerate(tp_peers):
        start(remote(final.at[t], final.at[t], kys.at[i], kyr.at[i], (a, f, peer)))
    for i in range(3):
        peer = lax.rem(t + 3 - i, 4)
        remote(final.at[peer], final.at[peer], kys.at[i], kyr.at[i], (a, f, peer)).wait_recv()
    for other in range(4):
        for source in range(8):
            stream_out[:, pl.ds((source * 4 + other) * HD, HD)] = final[other, source]
    for copy in sent:
        copy.wait_send()


VMEM = pl.BlockSpec(memory_space=pltpu.VMEM)
ANY = pl.BlockSpec(memory_space=pl.ANY)
DMA = pltpu.SemaphoreType.DMA


def project(*operands):
    return pl.pallas_call(
        project_kernel,
        name="project",
        out_shape=(
            jax.ShapeDtypeStruct((512, HD), BF),
            jax.ShapeDtypeStruct((256, HD), F32),
            jax.ShapeDtypeStruct((256, 512), BF),
            jax.ShapeDtypeStruct((8, 128), F32),
            jax.ShapeDtypeStruct((8, 128), jnp.int32),
        ),
        in_specs=[ANY, ANY, ANY, VMEM, VMEM, ANY, ANY],
        out_specs=[VMEM] * 5,
        scratch_shapes=[
            pltpu.VMEM((32, 1024), BF),
            pltpu.VMEM((32, 128, HD), BF),
            pltpu.VMEM((32, 128, HD), BF),
            pltpu.VMEM((4096, HD), BF),
            pltpu.VMEM((8, 4, 32, 1024), BF),
            pltpu.VMEM((8, 32, HD), BF),
            pltpu.VMEM((8, 1, 256), jnp.int32),
            pltpu.VMEM((512, 256), BF),
            pltpu.VMEM((8, 64, HD), BF),
            pltpu.VMEM((8, 64, HD), BF),
            pltpu.VMEM((1, 128), F32),
            pltpu.VMEM((8, 1, 128), F32),
            DMA((4,)),
            *[DMA((7,)) for _ in range(8)],
            DMA(()),
            *GATHER_SEMS,
        ],
        compiler_params=pltpu.CompilerParams(
            collective_id=0, has_side_effects=True, vmem_limit_bytes=60 * 2**20
        ),
    )(*operands)


def feed_forward(rows, identity, *operands):
    return pl.pallas_call(
        functools.partial(ffn_kernel, rows),
        name=f"feed_forward_{rows}",
        out_shape=(
            jax.ShapeDtypeStruct((32, 4096), BF),
            jax.ShapeDtypeStruct((1, HD), F32),
        ),
        in_specs=[VMEM] * 5 + [ANY] * 3,
        out_specs=[VMEM] * 2,
        scratch_shapes=[
            pltpu.VMEM((448, 4096), BF),
            pltpu.VMEM((448, 4096), BF),
            pltpu.VMEM((448, 4096), BF),
            pltpu.VMEM((8, 4, rows + 16, HD), BF),
            pltpu.VMEM((rows, 448), F32),
            pltpu.VMEM((rows, 448), F32),
            pltpu.VMEM((rows, 448), BF),
            pltpu.VMEM((4, rows, 512), BF),
            pltpu.VMEM((4, rows, 512), BF),
            pltpu.VMEM((4, rows, 512), F32),
            pltpu.VMEM((4, 2, rows, HD), BF),
            pltpu.VMEM((4, 2, rows, HD), BF),
            pltpu.VMEM((4, 2, rows // 2, HD), BF),
            pltpu.VMEM((4, 2, rows // 2, HD), BF),
            pltpu.VMEM((3, rows, HD), BF),
            pltpu.VMEM((3, rows, HD), BF),
            pltpu.VMEM((512, rows), BF),
            pltpu.VMEM((8, 64, HD), BF),
            pltpu.VMEM((8, 64, HD), BF),
            pltpu.VMEM((4, 8, 32, HD), BF),
            pltpu.VMEM((8, 32, HD), BF),
            DMA((3,)),
            DMA((4,)),
            DMA((4,)),
            *[DMA((4, 2)) for _ in range(4)],
            DMA((3,)),
            DMA((3,)),
            *[DMA((7,)) for _ in range(4)],
            DMA((3,)),
            DMA((3,)),
            *GATHER_SEMS,
        ],
        compiler_params=pltpu.CompilerParams(
            collective_id=identity, has_side_effects=True, vmem_limit_bytes=56 * 2**20
        ),
    )(*operands)


def per_device(
    queries, keys, values, lengths, routes, residual, w_out, norm_gain, w_gate, w_up, w_down
):
    a = lax.axis_index("attn")
    lens = jnp.broadcast_to(lengths[:, None], (32, 128))
    code = jnp.where(lengths > 0, routes[:, 0], 8) + 1
    codes = jnp.where(iota((8, 32), 0) == a, code[None, :], 0).reshape(1, 256)
    h, hidden, back, table, need = project(queries, keys, values, lens, codes, residual, w_out)
    operands = (h, hidden, back, table, norm_gain[None, :], w_gate[0].T, w_up[0].T, w_down[0])
    return lax.cond(
        need[0, 0] <= 256,
        functools.partial(feed_forward, 256, 1),
        functools.partial(feed_forward, 512, 2),
        *operands,
    )


def solution(mesh):
    placed = (
        P(("attn", "ffn"), "tp"),
        P(("attn", "ffn"), None, "tp"),
        P(("attn", "ffn"), None, "tp"),
        P(("attn", "ffn")),
        P(("attn", "ffn"), None),
        P(("attn", "ffn"), None),
        P(None, ("attn", "tp")),
        P(("attn", "tp")),
        P("ffn", None, ("attn", "tp")),
        P("ffn", None, ("attn", "tp")),
        P("ffn", ("attn", "tp"), None),
    )
    return jax.shard_map(
        per_device,
        mesh=mesh,
        in_specs=placed,
        out_specs=(P(("attn", "ffn"), None), P("ffn", ("attn", "tp"))),
        check_vma=False,
    )
```

```python
import functools
import math

import jax
import jax.numpy as jnp
from jax import lax
from jax.experimental import pallas as pl
from jax.experimental.pallas import tpu as pltpu
from jax.sharding import PartitionSpec as P

HD = 128
EPSILON = 1e-05
MESH = pl.DeviceIdType.MESH
BF = jnp.bfloat16
F32 = jnp.float32
Z_ORDER = (1, 3, 2)
RS_ORDER = (2, 1, 3, 0)


def iota(shape, dim):
    return lax.broadcasted_iota(jnp.int32, shape, dim)


def position():
    return lax.axis_index("attn"), lax.axis_index("ffn"), lax.axis_index("tp")


def remote(src, dst, send, recv, device):
    return pltpu.make_async_remote_copy(
        src_ref=src, dst_ref=dst, send_sem=send, recv_sem=recv, device_id=device, device_id_type=MESH
    )


def greet(devices):
    barrier = pltpu.get_barrier_semaphore()
    for device in devices:
        pl.semaphore_signal(barrier, inc=1, device_id=device, device_id_type=MESH)
    return lambda: pl.semaphore_wait(barrier, len(devices))


def gather_group(buf, half, zs, zr, ys, yr, hs, hr, cs, cr, consume, meanwhile=None):
    a, f, t = position()
    right, left = lax.rem(t + 1, 4), lax.rem(t + 3, 4)
    opposite = lax.rem(t + 2, 4)
    sibling = a + 1 - 2 * lax.rem(a, 2)
    rows = buf.shape[2]
    first, second = pl.ds(0, half), pl.ds(half, rows - half)
    source = [a] + [lax.rem(a + 8 - 2 * dz, 8) for dz in Z_ORDER]
    sent = []

    def start(copy):
        copy.start()
        sent.append(copy)

    def z_send(k):
        start(remote(buf.at[a, t], buf.at[a, t], zs.at[k], zr.at[k], (lax.rem(a + 2 * Z_ORDER[k], 8), f, t)))

    def z_wait(k):
        slot = buf.at[source[k + 1], t]
        remote(slot, slot, zs.at[k], zr.at[k], (a, f, right)).wait_recv()

    def y_send(k):
        slot = buf.at[source[k], t]
        start(remote(slot, slot, ys.at[k, 0], yr.at[k, 0], (a, f, right)))
        start(remote(slot, slot, ys.at[k, 1], yr.at[k, 1], (a, f, left)))
        if k == 3:
            start(remote(slot, slot, hs.at[k, 0], hr.at[k, 0], (a, f, opposite)))

    def y_forward(k):
        slot = buf.at[source[k], left]
        remote(slot, slot, ys.at[k, 0], yr.at[k, 0], (a, f, right)).wait_recv()
        if k == 3:
            slot = buf.at[source[k], right]
            remote(slot, slot, ys.at[k, 1], yr.at[k, 1], (a, f, left)).wait_recv()
            return
        piece = slot.at[first]
        start(remote(piece, piece, hs.at[k, 0], hr.at[k, 0], (a, f, right)))
        slot = buf.at[source[k], right]
        remote(slot, slot, ys.at[k, 1], yr.at[k, 1], (a, f, left)).wait_recv()
        piece = slot.at[second]
        start(remote(piece, piece, hs.at[k, 1], hr.at[k, 1], (a, f, left)))

    def core_send(k):
        slot = buf.at[source[k], opposite]
        if k == 3:
            remote(slot, slot, hs.at[k, 0], hr.at[k, 0], (a, f, opposite)).wait_recv()
            chunk = buf.at[source[k]]
            start(remote(chunk, chunk, cs.at[k], cr.at[k], (sibling, f, t)))
            return
        remote(slot.at[first], slot.at[first], hs.at[k, 0], hr.at[k, 0], (a, f, right)).wait_recv()
        remote(slot.at[second], slot.at[second], hs.at[k, 1], hr.at[k, 1], (a, f, left)).wait_recv()
        chunk = buf.at[source[k]]
        start(remote(chunk, chunk, cs.at[k], cr.at[k], (sibling, f, t)))

    def core_wait(k):
        other = source[k] + 1 - 2 * lax.rem(a, 2)
        chunk = buf.at[other]
        remote(chunk, chunk, cs.at[k], cr.at[k], (sibling, f, t)).wait_recv()
        consume(lax.div(source[k], 2))

    for k in range(3):
        z_send(k)
    y_send(0)
    if meanwhile is not None:
        sent.extend(meanwhile())
    z_wait(0)
    y_send(1)
    y_forward(0)
    z_wait(1)
    y_send(2)
    y_forward(1)
    core_send(0)
    z_wait(2)
    y_send(3)
    y_forward(2)
    core_send(1)
    core_wait(0)
    y_forward(3)
    core_send(2)
    core_wait(1)
    core_send(3)
    core_wait(2)
    core_wait(3)
    return sent


GATHER_SEMS = [
    pltpu.SemaphoreType.DMA((3,)),
    pltpu.SemaphoreType.DMA((3,)),
    pltpu.SemaphoreType.DMA((4, 2)),
    pltpu.SemaphoreType.DMA((4, 2)),
    pltpu.SemaphoreType.DMA((4, 2)),
    pltpu.SemaphoreType.DMA((4, 2)),
    pltpu.SemaphoreType.DMA((4,)),
    pltpu.SemaphoreType.DMA((4,)),
]


def attend(q, k, v, lens, att):
    for part in range(2):
        base = part * 16
        heads = jnp.concatenate([q[base : base + 16, h * HD : (h + 1) * HD] for h in range(8)], axis=0)
        slot = lax.rem(iota((128, 128), 0), 16)
        scores = jnp.zeros((128, 128), F32)
        for pair in range(8):
            block = k[base + 2 * pair : base + 2 * pair + 2].reshape(256, HD)
            both = lax.dot_general(heads, block, (((1,), (1,)), ((), ())), preferred_element_type=F32)
            scores = jnp.where(slot == 2 * pair, both[:, :128], scores)
            scores = jnp.where(slot == 2 * pair + 1, both[:, 128:], scores)
        scores = scores / math.sqrt(HD)
        limit = jnp.concatenate([lens[base : base + 16, :]] * 8, axis=0)
        valid = iota((128, 128), 1) < limit
        top = jnp.max(jnp.where(valid, scores, -1e30), axis=-1, keepdims=True)
        unnormed = jnp.where(valid, jnp.exp(scores - top), 0.0)
        summed = jnp.maximum(jnp.sum(unnormed, axis=-1, keepdims=True), 1.0)
        weights = unnormed / summed
        total = jnp.zeros((128, HD), F32)
        for pair in range(8):
            block = v[base + 2 * pair : base + 2 * pair + 2].reshape(256, HD)
            masked = jnp.concatenate(
                [jnp.where(slot == 2 * pair, weights, 0.0), jnp.where(slot == 2 * pair + 1, weights, 0.0)], axis=1
            ).astype(BF)
            total = total + jnp.dot(masked, block, preferred_element_type=F32)
        total = total.astype(BF)
        for h in range(8):
            att[pl.ds(base, 16), pl.ds(h * HD, HD)] = total[h * 16 : (h + 1) * 16, :]


def project_kernel(
    q_hbm, k_hbm, v_hbm, len_hbm, route_hbm, res_hbm, wout_hbm,
    h_out, hidden, back_out, table_out, small_out,
    q, k, v, wout, lens, routes, wide, codes, buf, res, cbuf, place, sbuf, hbuf, tsend, tbuf,
    in_sems, rs, rr, es, er, fs, fr, gs, gr, own_sem, *gather_sems,
):
    a, f, t = position()
    attn_peers = [lax.rem(a + step, 8) for step in range(1, 8)]
    ffn_peers = [lax.rem(f + step, 8) for step in range(1, 8)]
    all_here = greet(
        [(peer, f, t) for peer in attn_peers]
        + [(a, peer, t) for peer in ffn_peers]
        + [(a, f, lax.rem(t + step, 4)) for step in range(1, 4)]
    )
    loads = []
    pairs = (
        (len_hbm, lens), (route_hbm, routes), (q_hbm, q), (k_hbm, k), (v_hbm, v), (wout_hbm, wout),
    )
    for i, (src, dst) in enumerate(pairs):
        copy = pltpu.make_async_copy(src, dst, in_sems.at[i])
        copy.start()
        loads.append(copy)

    def columns(index):
        return pl.ds(pl.multiple_of((index * 4 + t) * HD, HD), HD)

    loads[0].wait()
    loads[1].wait()
    wide[...] = jnp.zeros((8, 128), F32)
    wide[0:1, 0:32] = lens[...].astype(F32)
    wide[1:2, 0:32] = jnp.where(lens[...] > 0, routes[...], 8).astype(F32) + 1.0
    limits = jnp.broadcast_to(wide[0:1, :], (128, 128)).T[:32].astype(jnp.int32)
    tile = jnp.where(iota((128, 256), 0) == lax.rem(iota((128, 256), 1), 32), 1.0, 0.0).astype(BF)
    tiled = jnp.dot(jnp.broadcast_to(wide[1:2, :], (16, 128)).astype(BF), tile, preferred_element_type=F32)
    codes[...] = jnp.where(iota((1, 256), 1) // 32 == a, tiled[:1], 0.0)
    for copy in loads[2:5]:
        copy.wait()
    attend(q, k, v, limits, buf.at[a, t])
    cbuf[a] = codes[...]
    own = pltpu.make_async_copy(res_hbm.at[:, columns(a)], res.at[a], own_sem)
    own.start()
    all_here()

    def exchange():
        sent = []
        for i, peer in enumerate(attn_peers):
            copy = remote(codes, cbuf.at[a], es.at[i], er.at[i], (peer, f, t))
            copy.start()
            sent.append(copy)
            copy = remote(res_hbm.at[:, columns(peer)], res.at[a], rs.at[i], rr.at[i], (peer, f, t))
            copy.start()
            sent.append(copy)
        return sent

    def prepare():
        loads[5].wait()
        own.wait()
        for i in range(7):
            peer = lax.rem(a + 7 - i, 8)
            remote(cbuf.at[peer], cbuf.at[peer], es.at[i], er.at[i], (peer, f, t)).wait_recv()
        code = cbuf[0]
        for i in range(1, 8):
            code = code + cbuf[i]
        code = code - 1.0
        code_t = jnp.broadcast_to(code, (256, 256)).T
        down, across = iota((256, 256), 0), iota((256, 256), 1)
        same = (code_t == code) & (down // 32 == across // 32)
        rank_row = jnp.sum(jnp.where(same & (down < across), 1.0, 0.0), axis=0, keepdims=True)
        rank_col = jnp.sum(jnp.where(same & (across < down), 1.0, 0.0), axis=1, keepdims=True)
        target_row = (code * 8.0 + rank_row).astype(jnp.int32)
        target_col = (code_t[:, 0:1] * 8.0 + rank_col).astype(jnp.int32)
        p, q_index = iota((512, 64), 0), iota((512, 64), 1)
        wanted = (lax.rem(p, 128) // 16) * 8 + lax.rem(p, 8)
        of_z = jnp.concatenate(
            [jnp.broadcast_to(target_row[:, z * 64 : (z + 1) * 64], (128, 64)) for z in range(4)], axis=0
        )
        hit = (wanted == of_z) & (lax.rem(p // 8, 2) == q_index // 32)
        place[...] = jnp.where(hit, 1.0, 0.0).astype(BF).reshape(4, 128, 64)
        q_index, p = iota((256, 512), 0), iota((256, 512), 1)
        hit = ((p // 64) * 8 + lax.rem(p, 8) == target_col) & (lax.rem(p // 8, 8) == q_index // 32)
        back_out[...] = jnp.where(hit, 1.0, 0.0).astype(BF)
        q_index, j = iota((256, 128), 0), iota((256, 128), 1)
        block = (q_index // 32 == lax.rem(j, 8)) & (j < 64)
        named = (code_t[:, :128] == (j // 8).astype(F32)) & block
        tsend[...] = jnp.sum(jnp.where(named, 1.0, 0.0), axis=0, keepdims=True)
        tbuf[f] = tsend[...]
        for i in range(7):
            peer = lax.rem(a + 7 - i, 8)
            remote(res.at[peer], res.at[peer], rs.at[i], rr.at[i], (peer, f, t)).wait_recv()

    later = []
    chunks = []

    def consume(z):
        if not chunks:
            prepare()
            for i, peer in enumerate(ffn_peers):
                copy = remote(tsend, tbuf.at[f], gs.at[i], gr.at[i], (a, peer, t))
                copy.start()
                later.append(copy)
        number = len(chunks)
        chunks.append(z)
        pair = pl.ds(2 * z, 2)
        total = jnp.zeros((64, HD), F32)
        for other in range(4):
            left = buf[pair, other].reshape(64, 1024)
            total = total + jnp.dot(left, wout[pl.ds(other * 1024, 1024), :], preferred_element_type=F32)
        total = total + res[pair].reshape(64, HD).astype(F32)
        hidden[pl.ds(pl.multiple_of(z * 64, 64), 64), :] = total
        routed = jnp.dot(place[z], total.astype(BF), preferred_element_type=F32).astype(BF)
        sbuf[z] = routed.reshape(8, 16, HD)
        for i, peer in enumerate(ffn_peers):
            copy = remote(sbuf.at[z, peer], hbuf.at[f, z], fs.at[number, i], fr.at[number, i], (a, peer, t))
            copy.start()
            later.append(copy)
        hbuf[f, z] = sbuf[z, f]

    sent = gather_group(buf, 16, *gather_sems, consume, exchange)
    sent += later
    for i in range(7):
        peer = lax.rem(f + 7 - i, 8)
        remote(tbuf.at[peer], tbuf.at[peer], gs.at[i], gr.at[i], (a, peer, t)).wait_recv()
    table = tbuf[...].reshape(8, 128)
    table_out[...] = table
    sums = jnp.broadcast_to(jnp.sum(table, axis=0, keepdims=True), (16, 128)).astype(BF)
    fold = jnp.where(iota((128, 128), 0) // 8 == iota((128, 128), 1), 1.0, 0.0).astype(BF)
    totals = jnp.dot(sums, fold, preferred_element_type=F32)
    small_out[0, 0] = jnp.where(jnp.max(totals) <= 256.0, 1, 0)
    for number, z in enumerate(chunks):
        for i in range(7):
            peer = lax.rem(f + 7 - i, 8)
            slot = hbuf.at[peer, z]
            remote(slot, slot, fs.at[number, i], fr.at[number, i], (a, peer, t)).wait_recv()
    h_out[...] = hbuf[...].reshape(512, HD)
    for copy in sent:
        copy.wait_send()


def ffn_kernel(
    rows,
    h_ref, hidden, back, table, gain, wg_hbm, wu_hbm, wd_hbm,
    stream_out, sums_out,
    wg, wu, wd, buf, gate, up, act, csend, crecv, part, y1s, y1r, y2s, y2r, zsend, zrecv, unplace, rsend, rbuf, final,
    line, in_sems, kcs, kcr, k1s, k1r, k2s, k2r, kzs, kzr, kbs, kbr, kas, kar, kys, kyr, *gather_sems,
):
    a, f, t = position()
    z, core = lax.div(a, 2), lax.rem(a, 2)
    right, left, opposite = lax.rem(t + 1, 4), lax.rem(t + 3, 4), lax.rem(t + 2, 4)
    sibling = a + 1 - 2 * core
    half = rows // 2
    blocks = rows // 128
    loads = []
    for i, (src, dst) in enumerate(((wg_hbm, wg), (wu_hbm, wu), (wd_hbm, wd))):
        copy = pltpu.make_async_copy(src, dst, in_sems.at[i])
        copy.start()
        loads.append(copy)
    attn_peers = [lax.rem(a + step, 8) for step in range(1, 8)]
    ffn_peers = [lax.rem(f + step, 8) for step in range(1, 8)]
    tp_peers = [lax.rem(t + step, 4) for step in range(1, 4)]

    all_here = greet(
        [(peer, f, t) for peer in attn_peers]
        + [(a, peer, t) for peer in ffn_peers]
        + [(a, f, peer) for peer in tp_peers]
    )

    j, p = iota((128, 512), 0), iota((128, 512), 1)
    pick = jnp.where(j == f * 8 + lax.rem(p // 8, 8), 1.0, 0.0).astype(BF)
    table16 = jnp.concatenate([table[...], table[...]], axis=0).astype(BF)
    counts = jnp.dot(table16, pick, preferred_element_type=F32)[:8]
    s, p = iota((8, 512), 0), iota((8, 512), 1)
    counts = jnp.sum(jnp.where(s == p // 64, counts, 0.0), axis=0, keepdims=True)
    live = lax.rem(iota((1, 512), 1), 8).astype(F32) < counts
    flags = jnp.broadcast_to(jnp.where(live, 1.0, 0.0), (16, 512)).astype(BF)
    before = jnp.where(iota((512, 512), 0) < iota((512, 512), 1), 1.0, 0.0).astype(BF)
    place = jnp.dot(flags, before, preferred_element_type=F32)[:1]
    place = jnp.where(live, place, -1.0).astype(jnp.int32)
    compact = jnp.where(iota((rows, 512), 0) == place, 1.0, 0.0).astype(BF)
    picked = jnp.dot(compact, h_ref[...], preferred_element_type=F32)
    slot = buf.at[a, t]
    slot[pl.ds(0, rows), :] = (picked * gain[...]).astype(BF)
    squares = picked * picked
    tail = jnp.zeros((16, 128), F32)
    line_index = iota((16, 128), 0)
    for i in range(blocks):
        block = jnp.sum(squares[i * 128 : (i + 1) * 128].T, axis=0, keepdims=True)
        high = block.astype(BF).astype(F32)
        tail = jnp.where(line_index == i, high, tail)
        tail = jnp.where(line_index == blocks + i, block - high, tail)
    slot[pl.ds(rows, 16), :] = tail.astype(BF)

    all_here()

    first = [True]

    def consume(chunk):
        if first[0]:
            loads[0].wait()
            loads[1].wait()
            place_t = jnp.broadcast_to(place.astype(F32), (128, 512)).T.astype(jnp.int32)
            for i in range(blocks):
                hit = place_t == iota((512, 128), 1) + i * 128
                unplace[:, pl.ds(i * 128, 128)] = jnp.where(hit, 1.0, 0.0).astype(BF)
        for c in range(2):
            index = chunk * 2 + c
            depth = pl.ds(pl.multiple_of(index * 512, 512), 512)
            for m in range(0, rows, 256):
                span = pl.ds(m, 256)
                lhs = jnp.concatenate([buf[index, other, span, :] for other in range(4)], axis=1)
                for weight, total in ((wg, gate), (wu, up)):
                    value = lax.dot_general(
                        lhs, weight[:, depth], (((1,), (1,)), ((), ())), preferred_element_type=F32
                    )
                    if first[0] and c == 0:
                        total[span, :] = value
                    else:
                        total[span, :] += value
        first[0] = False

    sent = gather_group(buf, half + 16, *gather_sems, consume)

    tails = jnp.sum(buf[:, :, pl.ds(rows, 16), :].astype(F32).reshape(32, 16, 128), axis=0)
    for i in range(blocks):
        span = pl.ds(i * 128, 128)
        total = tails[i : i + 1] + tails[blocks + i : blocks + i + 1]
        inverse = lax.rsqrt(total / 4096.0 + EPSILON)
        scale = jnp.broadcast_to(inverse, (128, 128)).T
        scale = jnp.concatenate([scale] * 4, axis=1)[:, :448]
        g = gate[span, :] * scale
        act[span, :] = (g / (1.0 + jnp.exp(-g)) * (up[span, :] * scale)).astype(BF)
    loads[2].wait()

    def start(copy):
        copy.start()
        sent.append(copy)

    def chunk_columns(dz, c):
        index = lax.rem(z + dz, 4) * 2 + c
        return pl.ds(pl.multiple_of(index * 512, 512), 512)

    def down(dz, c, store):
        for m in range(0, rows, 256):
            span = pl.ds(m, 256)
            store(span, jnp.dot(act[span, :], wd[:, chunk_columns(dz, c)], preferred_element_type=F32))

    def give(i):
        def store(span, value):
            csend[i, span, :] = value.astype(BF)

        down(RS_ORDER[i], 1 - core, store)
        start(remote(csend.at[i], crecv.at[i], kcs.at[i], kcr.at[i], (sibling, f, t)))

    def keep(i):
        def store(span, value):
            part[i, span, :] = value

        down(RS_ORDER[i], core, store)

    def lanes(index):
        return pl.ds(pl.multiple_of(index * HD, HD), HD)

    top, low = pl.ds(0, half), pl.ds(half, half)

    def y_first(i):
        remote(csend.at[i], crecv.at[i], kcs.at[i], kcr.at[i], (sibling, f, t)).wait_recv()
        part[i] += crecv[i].astype(F32)
        y1s[i, 0, top, :] = part[i, top, lanes(opposite)].astype(BF)
        y1s[i, 0, low, :] = part[i, low, lanes(right)].astype(BF)
        start(remote(y1s.at[i, 0], y1r.at[i, 0], k1s.at[i, 0], k1r.at[i, 0], (a, f, right)))
        y1s[i, 1, top, :] = part[i, top, lanes(left)].astype(BF)
        y1s[i, 1, low, :] = part[i, low, lanes(opposite)].astype(BF)
        start(remote(y1s.at[i, 1], y1r.at[i, 1], k1s.at[i, 1], k1r.at[i, 1], (a, f, left)))

    def y_second(i):
        remote(y1s.at[i, 0], y1r.at[i, 0], k1s.at[i, 0], k1r.at[i, 0], (a, f, right)).wait_recv()
        y2s[i, 0] = (part[i, top, lanes(right)] + y1r[i, 0, top, :].astype(F32)).astype(BF)
        start(remote(y2s.at[i, 0], y2r.at[i, 0], k2s.at[i, 0], k2r.at[i, 0], (a, f, right)))
        remote(y1s.at[i, 1], y1r.at[i, 1], k1s.at[i, 1], k1r.at[i, 1], (a, f, left)).wait_recv()
        y2s[i, 1] = (part[i, low, lanes(left)] + y1r[i, 1, low, :].astype(F32)).astype(BF)
        start(remote(y2s.at[i, 1], y2r.at[i, 1], k2s.at[i, 1], k2r.at[i, 1], (a, f, left)))

    def y_sum(i):
        remote(y2s.at[i, 0], y2r.at[i, 0], k2s.at[i, 0], k2r.at[i, 0], (a, f, right)).wait_recv()
        remote(y2s.at[i, 1], y2r.at[i, 1], k2s.at[i, 1], k2r.at[i, 1], (a, f, left)).wait_recv()
        upper = part[i, top, lanes(t)] + y1r[i, 1, top, :].astype(F32) + y2r[i, 0].astype(F32)
        lower = part[i, low, lanes(t)] + y1r[i, 0, low, :].astype(F32) + y2r[i, 1].astype(F32)
        return upper, lower

    def z_give(i):
        dz = RS_ORDER[i]
        upper, lower = y_sum(i)
        zsend[i, top, :] = upper.astype(BF)
        zsend[i, low, :] = lower.astype(BF)
        start(remote(zsend.at[i], zrecv.at[i], kzs.at[i], kzr.at[i], (lax.rem(a + 2 * dz, 8), f, t)))

    give(0)
    keep(0)
    give(1)
    keep(1)
    y_first(0)
    give(2)
    keep(2)
    y_first(1)
    give(3)
    y_second(0)
    keep(3)
    y_first(2)
    y_second(1)
    y_first(3)
    z_give(0)
    y_second(2)
    z_give(1)
    y_second(3)
    z_give(2)
    total = jnp.concatenate(y_sum(3), axis=0)
    for i in range(3):
        remote(zsend.at[i], zrecv.at[i], kzs.at[i], kzr.at[i], (sibling, f, t)).wait_recv()
        total = total + zrecv[i].astype(F32)

    sums_out[...] = jnp.sum(total, axis=0, keepdims=True)
    spread = jnp.dot(unplace[...], total.astype(BF), preferred_element_type=F32).astype(BF)
    rsend[...] = spread.reshape(8, 64, HD)
    for i, peer in enumerate(ffn_peers):
        start(remote(rsend.at[peer], rbuf.at[f], kbs.at[i], kbr.at[i], (a, peer, t)))
    rbuf[f] = rsend[f]
    live_rows = jnp.sum(back[...].astype(F32), axis=1, keepdims=True) > 0.5
    for i in range(7):
        peer = lax.rem(f + 7 - i, 8)
        remote(rbuf.at[peer], rbuf.at[peer], kbs.at[i], kbr.at[i], (a, peer, t)).wait_recv()
    returned = jnp.dot(back[...], rbuf[...].reshape(512, HD), preferred_element_type=F32)
    line[...] = jnp.where(live_rows, hidden[...] + returned, 0.0).astype(BF).reshape(8, 32, HD)
    for step in (0, 1, 3, 2):
        for cross in (1, 0):
            if step or cross:
                peer = lax.rem(z + step, 4) * 2 + (1 - core if cross else core)
                copy = remote(
                    line.at[peer], final.at[t, a], kas.at[step, cross], kar.at[step, cross], (peer, f, t)
                )
                start(copy)
    final[t, a] = line[a]
    for step in (0, 1, 3, 2):
        from_z = lax.rem(z + 4 - step, 4)
        for cross in (1, 0):
            if step or cross:
                slot = final.at[t, from_z * 2 + (1 - core if cross else core)]
                remote(slot, slot, kas.at[step, cross], kar.at[step, cross], (sibling, f, t)).wait_recv()
        slot = final.at[t, pl.ds(2 * from_z, 2)]
        for i, peer in enumerate(tp_peers):
            start(remote(slot, slot, kys.at[step, i], kyr.at[step, i], (a, f, peer)))
    for step in (0, 1, 3, 2):
        from_z = lax.rem(z + 4 - step, 4)
        for i in range(3):
            peer = lax.rem(t + 3 - i, 4)
            slot = final.at[peer, pl.ds(2 * from_z, 2)]
            remote(slot, slot, kys.at[step, i], kyr.at[step, i], (a, f, peer)).wait_recv()
    for other in range(4):
        for source in range(8):
            stream_out[:, pl.ds((source * 4 + other) * HD, HD)] = final[other, source]
    for copy in sent:
        copy.wait_send()


VMEM = pl.BlockSpec(memory_space=pltpu.VMEM)
ANY = pl.BlockSpec(memory_space=pl.ANY)
DMA = pltpu.SemaphoreType.DMA


def project(*operands):
    return pl.pallas_call(
        project_kernel,
        name="project",
        out_shape=(
            jax.ShapeDtypeStruct((512, HD), BF),
            jax.ShapeDtypeStruct((256, HD), F32),
            jax.ShapeDtypeStruct((256, 512), BF),
            jax.ShapeDtypeStruct((8, 128), F32),
            jax.ShapeDtypeStruct((1, 1), jnp.int32),
        ),
        in_specs=[ANY] * 7,
        out_specs=[VMEM] * 4 + [pl.BlockSpec(memory_space=pltpu.SMEM)],
        scratch_shapes=[
            pltpu.VMEM((32, 1024), BF),
            pltpu.VMEM((32, 128, HD), BF),
            pltpu.VMEM((32, 128, HD), BF),
            pltpu.VMEM((4096, HD), BF),
            pltpu.VMEM((1, 32), jnp.int32),
            pltpu.VMEM((1, 32), jnp.int32),
            pltpu.VMEM((8, 128), F32),
            pltpu.VMEM((1, 256), F32),
            pltpu.VMEM((8, 4, 32, 1024), BF),
            pltpu.VMEM((8, 32, HD), BF),
            pltpu.VMEM((8, 1, 256), F32),
            pltpu.VMEM((4, 128, 64), BF),
            pltpu.VMEM((4, 8, 16, HD), BF),
            pltpu.VMEM((8, 4, 16, HD), BF),
            pltpu.VMEM((1, 128), F32),
            pltpu.VMEM((8, 1, 128), F32),
            DMA((6,)),
            *[DMA((7,)) for _ in range(4)],
            DMA((4, 7)),
            DMA((4, 7)),
            DMA((7,)),
            DMA((7,)),
            DMA(()),
            *GATHER_SEMS,
        ],
        compiler_params=pltpu.CompilerParams(
            collective_id=0, has_side_effects=True, vmem_limit_bytes=60 * 2**20
        ),
    )(*operands)


def feed_forward(rows, identity, *operands):
    return pl.pallas_call(
        functools.partial(ffn_kernel, rows),
        name=f"feed_forward_{rows}",
        out_shape=(
            jax.ShapeDtypeStruct((32, 4096), BF),
            jax.ShapeDtypeStruct((1, HD), F32),
        ),
        in_specs=[VMEM] * 5 + [ANY] * 3,
        out_specs=[VMEM] * 2,
        scratch_shapes=[
            pltpu.VMEM((448, 4096), BF),
            pltpu.VMEM((448, 4096), BF),
            pltpu.VMEM((448, 4096), BF),
            pltpu.VMEM((8, 4, rows + 16, HD), BF),
            pltpu.VMEM((rows, 448), F32),
            pltpu.VMEM((rows, 448), F32),
            pltpu.VMEM((rows, 448), BF),
            pltpu.VMEM((4, rows, 512), BF),
            pltpu.VMEM((4, rows, 512), BF),
            pltpu.VMEM((4, rows, 512), F32),
            pltpu.VMEM((4, 2, rows, HD), BF),
            pltpu.VMEM((4, 2, rows, HD), BF),
            pltpu.VMEM((4, 2, rows // 2, HD), BF),
            pltpu.VMEM((4, 2, rows // 2, HD), BF),
            pltpu.VMEM((3, rows, HD), BF),
            pltpu.VMEM((3, rows, HD), BF),
            pltpu.VMEM((512, rows), BF),
            pltpu.VMEM((8, 64, HD), BF),
            pltpu.VMEM((8, 64, HD), BF),
            pltpu.VMEM((4, 8, 32, HD), BF),
            pltpu.VMEM((8, 32, HD), BF),
            DMA((3,)),
            DMA((4,)),
            DMA((4,)),
            *[DMA((4, 2)) for _ in range(4)],
            DMA((3,)),
            DMA((3,)),
            DMA((7,)),
            DMA((7,)),
            DMA((4, 2)),
            DMA((4, 2)),
            DMA((4, 3)),
            DMA((4, 3)),
            *GATHER_SEMS,
        ],
        compiler_params=pltpu.CompilerParams(
            collective_id=identity, has_side_effects=True, vmem_limit_bytes=56 * 2**20
        ),
    )(*operands)


def per_device(
    queries, keys, values, lengths, routes, residual, w_out, norm_gain, w_gate, w_up, w_down
):
    h, hidden, back, table, small = project(
        queries, keys, values, lengths.reshape(1, 32), routes.reshape(1, 32), residual, w_out
    )
    operands = (h, hidden, back, table, norm_gain[None, :], w_gate[0].T, w_up[0].T, w_down[0])
    return lax.cond(
        small[0, 0] == 1,
        functools.partial(feed_forward, 256, 1),
        functools.partial(feed_forward, 512, 2),
        *operands,
    )


def solution(mesh):
    placed = (
        P(("attn", "ffn"), "tp"),
        P(("attn", "ffn"), None, "tp"),
        P(("attn", "ffn"), None, "tp"),
        P(("attn", "ffn")),
        P(("attn", "ffn"), None),
        P(("attn", "ffn"), None),
        P(None, ("attn", "tp")),
        P(("attn", "tp")),
        P("ffn", None, ("attn", "tp")),
        P("ffn", None, ("attn", "tp")),
        P("ffn", ("attn", "tp"), None),
    )
    return jax.shard_map(
        per_device,
        mesh=mesh,
        in_specs=placed,
        out_specs=(P(("attn", "ffn"), None), P("ffn", ("attn", "tp"))),
        check_vma=False,
    )
```

```python
import functools
import math
import types

import jax
import jax.numpy as jnp
from jax import lax
from jax.experimental import pallas as pl
from jax.experimental.pallas import tpu as pltpu
from jax.sharding import PartitionSpec as P

HD = 128
EPSILON = 1e-05
MESH = pl.DeviceIdType.MESH
BF = jnp.bfloat16
F32 = jnp.float32
Z_ORDER = (1, 3, 2)
RS_ORDER = (2, 1, 3, 0)


def iota(shape, dim):
    return lax.broadcasted_iota(jnp.int32, shape, dim)


def position():
    return lax.axis_index("attn"), lax.axis_index("ffn"), lax.axis_index("tp")


def remote(src, dst, send, recv, device):
    return pltpu.make_async_remote_copy(
        src_ref=src, dst_ref=dst, send_sem=send, recv_sem=recv, device_id=device, device_id_type=MESH
    )


def greet(devices):
    barrier = pltpu.get_barrier_semaphore()
    for device in devices:
        pl.semaphore_signal(barrier, inc=1, device_id=device, device_id_type=MESH)
    return lambda: pl.semaphore_wait(barrier, len(devices))


def gather_group(buf, half, zs, zr, ys, yr, hs, hr, cs, cr, consume, meanwhile=None):
    a, f, t = position()
    right, left = lax.rem(t + 1, 4), lax.rem(t + 3, 4)
    opposite = lax.rem(t + 2, 4)
    sibling = a + 1 - 2 * lax.rem(a, 2)
    rows = buf.shape[2]
    pieces = (pl.ds(0, half), pl.ds(half, rows - half))
    source = [a] + [lax.rem(a + 8 - 2 * dz, 8) for dz in Z_ORDER]
    sent = []

    def start(copy):
        copy.start()
        sent.append(copy)

    def z_send(k, h):
        piece = buf.at[a, t].at[pieces[h]]
        start(remote(piece, piece, zs.at[k, h], zr.at[k, h], (lax.rem(a + 2 * Z_ORDER[k], 8), f, t)))

    def z_wait(k, h):
        piece = buf.at[source[k + 1], t].at[pieces[h]]
        remote(piece, piece, zs.at[k, h], zr.at[k, h], (a, f, right)).wait_recv()

    def z_forward(h):
        piece = buf.at[source[2 if h else 1], t].at[pieces[h]]
        z = lax.rem(a + (6 if h else 2), 8)
        start(remote(piece, piece, zs.at[2, h], zr.at[2, h], (z, f, t)))

    def y_copy(k, slot, h, way):
        piece = buf.at[source[k], slot].at[pieces[h]]
        return remote(piece, piece, ys.at[k, way, h], yr.at[k, way, h], (a, f, left if way else right))

    def y_send(k, h):
        start(y_copy(k, t, h, h))
        start(y_copy(k, t, h, 1 - h))
        if k == 3:
            piece = buf.at[source[k], t].at[pieces[h]]
            start(remote(piece, piece, hs.at[k, h], hr.at[k, h], (a, f, opposite)))

    def y_forward(k):
        if k == 3:
            return
        for h in range(2):
            slot = right if h else left
            y_copy(k, slot, h, h).wait_recv()
            piece = buf.at[source[k], slot].at[pieces[h]]
            start(remote(piece, piece, hs.at[k, h], hr.at[k, h], (a, f, left if h else right)))

    def core_send(k):
        if k == 3:
            for h in range(2):
                y_copy(k, right if h else left, h, h).wait_recv()
        for h in range(2):
            y_copy(k, left if h else right, h, 1 - h).wait_recv()
        for h in range(2):
            piece = buf.at[source[k], opposite].at[pieces[h]]
            remote(piece, piece, hs.at[k, h], hr.at[k, h], (a, f, right)).wait_recv()
        chunk = buf.at[source[k]]
        start(remote(chunk, chunk, cs.at[k], cr.at[k], (sibling, f, t)))

    def core_wait(k):
        other = source[k] + 1 - 2 * lax.rem(a, 2)
        chunk = buf.at[other]
        remote(chunk, chunk, cs.at[k], cr.at[k], (sibling, f, t)).wait_recv()
        consume(lax.div(source[k], 2))

    z_send(0, 0)
    z_send(1, 1)
    z_send(0, 1)
    z_send(1, 0)
    y_send(0, 0)
    y_send(0, 1)
    if meanwhile is not None:
        sent.extend(meanwhile())
    z_wait(0, 0)
    z_forward(0)
    y_send(1, 0)
    z_wait(1, 1)
    z_forward(1)
    y_send(2, 1)
    z_wait(0, 1)
    y_send(1, 1)
    z_wait(1, 0)
    y_send(2, 0)
    y_forward(0)
    for h in range(2):
        z_wait(2, h)
        y_send(3, h)
    y_forward(1)
    y_forward(2)
    core_send(0)
    core_send(1)
    core_wait(0)
    y_forward(3)
    core_send(2)
    core_wait(1)
    core_send(3)
    core_wait(2)
    core_wait(3)
    return sent


GATHER_SEMS = [
    pltpu.SemaphoreType.DMA((3, 2)),
    pltpu.SemaphoreType.DMA((3, 2)),
    pltpu.SemaphoreType.DMA((4, 2, 2)),
    pltpu.SemaphoreType.DMA((4, 2, 2)),
    pltpu.SemaphoreType.DMA((4, 2)),
    pltpu.SemaphoreType.DMA((4, 2)),
    pltpu.SemaphoreType.DMA((4,)),
    pltpu.SemaphoreType.DMA((4,)),
]


def scatter_group(give, keep, r, settle):
    a, f, t = position()
    right, left, opposite = lax.rem(t + 1, 4), lax.rem(t + 3, 4), lax.rem(t + 2, 4)
    sibling = a + 1 - 2 * lax.rem(a, 2)
    csend, crecv, part, y1s, y1r, y2s, y2r, zsend, zrecv = (
        r.csend, r.crecv, r.part, r.y1s, r.y1r, r.y2s, r.y2r, r.zsend, r.zrecv
    )
    half = part.shape[1] // 2
    halves = (pl.ds(0, half), pl.ds(half, half))
    sent = []

    def start(copy):
        copy.start()
        sent.append(copy)

    def block(i, span, index):
        lanes = pl.ds(pl.multiple_of(index * HD, HD), HD)
        return part[i, span, lanes] + crecv[i, span, lanes].astype(F32)

    def core_copy(i):
        return remote(csend.at[i], crecv.at[i], r.kcs.at[i], r.kcr.at[i], (sibling, f, t))

    def first_copy(i, way, h):
        src, dst = y1s.at[i, way, halves[h]], y1r.at[i, way, halves[h]]
        return remote(src, dst, r.k1s.at[i, way, h], r.k1r.at[i, way, h], (a, f, left if way else right))

    def second_copy(i, way):
        device = (a, f, left if way else right)
        return remote(y2s.at[i, way], y2r.at[i, way], r.k2s.at[i, way], r.k2r.at[i, way], device)

    def z_copy(i, h):
        src, dst = zsend.at[i, halves[h]], zrecv.at[i, halves[h]]
        return remote(src, dst, r.kzs.at[i, h], r.kzr.at[i, h], (lax.rem(a + 2 * RS_ORDER[i], 8), f, t))

    def core_give(i):
        give(i)
        start(core_copy(i))
        keep(i)

    def y_first(i):
        core_copy(i).wait_recv()
        for way in range(2):
            y1s[i, way, halves[way], :] = block(i, halves[way], opposite).astype(BF)
            start(first_copy(i, way, way))
        for way in range(2):
            span = halves[1 - way]
            y1s[i, way, span, :] = block(i, span, left if way else right).astype(BF)
            start(first_copy(i, way, 1 - way))

    def y_second(i):
        for way in range(2):
            value = block(i, halves[way], left if way else right)
            first_copy(i, way, way).wait_recv()
            y2s[i, way] = (value + y1r[i, way, halves[way], :].astype(F32)).astype(BF)
            start(second_copy(i, way))

    def y_sum(i, h):
        value = block(i, halves[h], t)
        first_copy(i, 1 - h, h).wait_recv()
        value = value + y1r[i, 1 - h, halves[h], :].astype(F32)
        second_copy(i, h).wait_recv()
        return value + y2r[i, h].astype(F32)

    def z_give(i):
        for h in range(2):
            zsend[i, halves[h], :] = y_sum(i, h).astype(BF)
            start(z_copy(i, h))

    core_give(0)
    core_give(1)
    y_first(0)
    core_give(2)
    y_first(1)
    y_second(0)
    core_give(3)
    y_first(2)
    y_second(1)
    y_first(3)
    settle()
    z_give(0)
    y_second(2)
    z_give(1)
    y_second(3)
    z_give(2)
    total = []
    for h in range(2):
        value = y_sum(3, h)
        for i in range(3):
            z_copy(i, h).wait_recv()
            value = value + zrecv[i, halves[h], :].astype(F32)
        total.append(value)
    return jnp.concatenate(total, axis=0), sent


def attend(q, k, v, lens, att):
    for part in range(2):
        base = part * 16
        heads = jnp.concatenate([q[base : base + 16, h * HD : (h + 1) * HD] for h in range(8)], axis=0)
        slot = lax.rem(iota((128, 128), 0), 16)
        scores = jnp.zeros((128, 128), F32)
        for pair in range(8):
            block = k[base + 2 * pair : base + 2 * pair + 2].reshape(256, HD)
            both = lax.dot_general(heads, block, (((1,), (1,)), ((), ())), preferred_element_type=F32)
            scores = jnp.where(slot == 2 * pair, both[:, :128], scores)
            scores = jnp.where(slot == 2 * pair + 1, both[:, 128:], scores)
        scores = scores / math.sqrt(HD)
        limit = jnp.concatenate([lens[base : base + 16, :]] * 8, axis=0)
        valid = iota((128, 128), 1) < limit
        top = jnp.max(jnp.where(valid, scores, -1e30), axis=-1, keepdims=True)
        unnormed = jnp.where(valid, jnp.exp(scores - top), 0.0)
        summed = jnp.maximum(jnp.sum(unnormed, axis=-1, keepdims=True), 1.0)
        weights = unnormed / summed
        total = jnp.zeros((128, HD), F32)
        for pair in range(8):
            block = v[base + 2 * pair : base + 2 * pair + 2].reshape(256, HD)
            masked = jnp.concatenate(
                [jnp.where(slot == 2 * pair, weights, 0.0), jnp.where(slot == 2 * pair + 1, weights, 0.0)], axis=1
            ).astype(BF)
            total = total + jnp.dot(masked, block, preferred_element_type=F32)
        total = total.astype(BF)
        for h in range(8):
            att[pl.ds(base, 16), pl.ds(h * HD, HD)] = total[h * 16 : (h + 1) * 16, :]


def project_part(r, peers):
    a, f, t = position()
    q, k, v, wout, lens, routes, wide, codes, buf, res = (
        r.q, r.k, r.v, r.wout, r.lens, r.routes, r.wide, r.codes, r.heads, r.res
    )
    cbuf, place, sbuf, hbuf, tsend, tbuf = r.cbuf, r.place, r.sbuf, r.hbuf, r.tsend, r.tbuf
    in_sems, rs, rr, es, er, fs, fr, gs, gr = r.in_sems, r.rs, r.rr, r.es, r.er, r.fs, r.fr, r.gs, r.gr
    back_out, res_hbm, hsend, hall = r.back, r.res_hbm, r.hsend, r.hall
    own_z, core = lax.div(a, 2), lax.rem(a, 2)
    attn_peers = [lax.rem(a + step, 8) for step in range(1, 8)]
    ffn_peers = [lax.rem(f + step, 8) for step in range(1, 8)]
    all_here = greet(peers)
    loads = []
    pairs = (
        (r.len_hbm, lens), (r.route_hbm, routes), (r.q_hbm, q), (r.k_hbm, k), (r.v_hbm, v), (r.wout_hbm, wout),
    )
    for i, (src, dst) in enumerate(pairs):
        copy = pltpu.make_async_copy(src, dst, in_sems.at[i])
        copy.start()
        loads.append(copy)

    def columns(index):
        return pl.ds(pl.multiple_of((index * 4 + t) * HD, HD), HD)

    loads[0].wait()
    loads[1].wait()
    wide[...] = jnp.zeros((8, 128), F32)
    wide[0:1, 0:32] = lens[...].astype(F32)
    wide[1:2, 0:32] = jnp.where(lens[...] > 0, routes[...], 8).astype(F32) + 1.0
    limits = jnp.broadcast_to(wide[0:1, :], (128, 128)).T[:32].astype(jnp.int32)
    tile = jnp.where(iota((128, 256), 0) == lax.rem(iota((128, 256), 1), 32), 1.0, 0.0).astype(BF)
    tiled = jnp.dot(jnp.broadcast_to(wide[1:2, :], (16, 128)).astype(BF), tile, preferred_element_type=F32)
    codes[...] = jnp.where(iota((1, 256), 1) // 32 == a, tiled[:1], 0.0)
    for copy in loads[2:5]:
        copy.wait()
    attend(q, k, v, limits, buf.at[a, t])
    cbuf[a] = codes[...]
    own = pltpu.make_async_copy(res_hbm.at[:, columns(a)], res.at[a], r.own_sem)
    own.start()
    all_here()

    def exchange():
        sent = []
        for i, peer in enumerate(attn_peers):
            copy = remote(codes, cbuf.at[a], es.at[i], er.at[i], (peer, f, t))
            copy.start()
            sent.append(copy)
            copy = remote(res_hbm.at[:, columns(peer)], res.at[a], rs.at[i], rr.at[i], (peer, f, t))
            copy.start()
            sent.append(copy)
        return sent

    def prepare():
        loads[5].wait()
        own.wait()
        for i in range(7):
            peer = lax.rem(a + 7 - i, 8)
            remote(cbuf.at[peer], cbuf.at[peer], es.at[i], er.at[i], (peer, f, t)).wait_recv()
        code = cbuf[0]
        for i in range(1, 8):
            code = code + cbuf[i]
        code = code - 1.0
        code_t = jnp.broadcast_to(code, (256, 256)).T
        down, across = iota((256, 256), 0), iota((256, 256), 1)
        same = (code_t == code) & (down // 32 == across // 32)
        rank_row = jnp.sum(jnp.where(same & (down < across), 1.0, 0.0), axis=0, keepdims=True)
        rank_col = jnp.sum(jnp.where(same & (across < down), 1.0, 0.0), axis=1, keepdims=True)
        target_row = (code * 8.0 + rank_row).astype(jnp.int32)
        target_col = (code_t[:, 0:1] * 8.0 + rank_col).astype(jnp.int32)
        p, q_index = iota((512, 64), 0), iota((512, 64), 1)
        wanted = (lax.rem(p, 128) // 16) * 8 + lax.rem(p, 8)
        of_z = jnp.concatenate(
            [jnp.broadcast_to(target_row[:, z * 64 : (z + 1) * 64], (128, 64)) for z in range(4)], axis=0
        )
        hit = (wanted == of_z) & (lax.rem(p // 8, 2) == q_index // 32)
        place[...] = jnp.where(hit, 1.0, 0.0).astype(BF).reshape(4, 128, 64)
        r.targets[...] = jnp.broadcast_to(target_col, (256, 128))
        own_targets = r.targets[pl.ds(pl.multiple_of(own_z * 64, 64), 64), :]
        q_index, p = iota((64, 128), 0), iota((64, 128), 1)
        hit = ((p // 16) * 8 + lax.rem(p, 8) == own_targets) & (lax.rem(p // 8, 2) == q_index // 32)
        back_out[...] = jnp.where(hit, 1.0, 0.0).astype(BF)
        q_index, j = iota((256, 128), 0), iota((256, 128), 1)
        block = (q_index // 32 == lax.rem(j, 8)) & (j < 64)
        named = (code_t[:, :128] == (j // 8).astype(F32)) & block
        tsend[...] = jnp.sum(jnp.where(named, 1.0, 0.0), axis=0, keepdims=True)
        tbuf[f] = tsend[...]
        for i in range(7):
            peer = lax.rem(a + 7 - i, 8)
            remote(res.at[peer], res.at[peer], rs.at[i], rr.at[i], (peer, f, t)).wait_recv()

    later = []
    chunks = []

    def consume(z):
        if not chunks:
            prepare()
            for i, peer in enumerate(ffn_peers):
                copy = remote(tsend, tbuf.at[f], gs.at[i], gr.at[i], (a, peer, t))
                copy.start()
                later.append(copy)
        number = len(chunks)
        chunks.append(z)
        pair = pl.ds(2 * z, 2)
        total = jnp.zeros((64, HD), F32)
        for other in range(4):
            left = buf[pair, other].reshape(64, 1024)
            total = total + jnp.dot(left, wout[pl.ds(other * 1024, 1024), :], preferred_element_type=F32)
        total = total + res[pair].reshape(64, HD).astype(F32)
        if number:
            hsend[z] = total
        else:
            hall[z] = total
        routed = jnp.dot(place[z], total.astype(BF), preferred_element_type=F32).astype(BF)
        sbuf[z] = routed.reshape(8, 16, HD)
        for i, peer in enumerate(ffn_peers):
            copy = remote(sbuf.at[z, peer], hbuf.at[f, z], fs.at[number, i], fr.at[number, i], (a, peer, t))
            copy.start()
            later.append(copy)
        hbuf[f, z] = sbuf[z, f]
        if number:
            copy = remote(hsend.at[z], hall.at[own_z], r.vs.at[number], r.vr.at[number], (z * 2 + core, f, t))
            copy.start()
            later.append(copy)

    sent = gather_group(buf, 16, *r.heads_sems, consume, exchange)
    for i in range(7):
        peer = lax.rem(f + 7 - i, 8)
        remote(tbuf.at[peer], tbuf.at[peer], gs.at[i], gr.at[i], (a, peer, t)).wait_recv()
    table = tbuf[...].reshape(8, 128)
    r.table[...] = table
    sums = jnp.broadcast_to(jnp.sum(table, axis=0, keepdims=True), (16, 128)).astype(BF)
    fold = jnp.where(iota((128, 128), 0) // 8 == iota((128, 128), 1), 1.0, 0.0).astype(BF)
    totals = jnp.dot(sums, fold, preferred_element_type=F32)
    r.small[0, 0] = jnp.where(jnp.max(totals) <= float(COMMON), 1, 0)
    positions(COMMON, r)
    for number, z in enumerate(chunks):
        for i in range(7):
            peer = lax.rem(f + 7 - i, 8)
            slot = hbuf.at[peer, z]
            remote(slot, slot, fs.at[number, i], fr.at[number, i], (a, peer, t)).wait_recv()
    r.h[...] = hbuf[...].reshape(512, HD)

    def finish():
        for i, dz in enumerate(Z_ORDER):
            slot = hall.at[lax.rem(own_z + dz, 4)]
            remote(slot, slot, r.vs.at[i + 1], r.vr.at[i + 1], (lax.rem(a + 2 * dz, 8), f, t)).wait_recv()
        r.hidden[...] = hall[...].reshape(256, HD)

    return sent + later, finish


def start_weights(r):
    loads = []
    for i, (src, dst) in enumerate(((r.wg_hbm, r.wg), (r.wu_hbm, r.wu), (r.wd_hbm, r.wd))):
        copy = pltpu.make_async_copy(src, dst, r.weight_sems.at[i])
        copy.start()
        loads.append(copy)
    return loads


def positions(rows, r):
    f = lax.axis_index("ffn")
    j, p = iota((128, 512), 0), iota((128, 512), 1)
    pick = jnp.where(j == f * 8 + lax.rem(p // 8, 8), 1.0, 0.0).astype(BF)
    table16 = jnp.concatenate([r.table[...], r.table[...]], axis=0).astype(BF)
    counts = jnp.dot(table16, pick, preferred_element_type=F32)[:8]
    s, p = iota((8, 512), 0), iota((8, 512), 1)
    counts = jnp.sum(jnp.where(s == p // 64, counts, 0.0), axis=0, keepdims=True)
    live = lax.rem(iota((1, 512), 1), 8).astype(F32) < counts
    flags = jnp.broadcast_to(jnp.where(live, 1.0, 0.0), (16, 512)).astype(BF)
    before = jnp.where(iota((512, 512), 0) < iota((512, 512), 1), 1.0, 0.0).astype(BF)
    place = jnp.dot(flags, before, preferred_element_type=F32)[:1]
    place = jnp.where(live, place, -1.0)
    r.compact[...] = jnp.where(iota((rows, 512), 0) == place.astype(jnp.int32), 1.0, 0.0).astype(BF)
    place_t = jnp.broadcast_to(place, (128, 512)).T.astype(jnp.int32)
    for i in range(rows // 128):
        hit = place_t == iota((512, 128), 1) + i * 128
        r.unplace[:, pl.ds(i * 128, 128)] = jnp.where(hit, 1.0, 0.0).astype(BF)


def ffn_part(rows, r, loads, pending, all_here, met, finish):
    a, f, t = position()
    hidden, back, gain, stream_out, sums_out = r.hidden, r.back, r.gain, r.stream, r.sums
    wg, wu, wd, buf, gate, up, act = r.wg, r.wu, r.wd, r.buf, r.gate, r.up, r.act
    csend, part, unplace, rsend, rbuf, final, line = r.csend, r.part, r.unplace, r.rsend, r.rbuf, r.final, r.line
    kbs, kbr, kys, kyr = r.kbs, r.kbr, r.kys, r.kyr
    z, core = lax.div(a, 2), lax.rem(a, 2)
    right, left, opposite = lax.rem(t + 1, 4), lax.rem(t + 3, 4), lax.rem(t + 2, 4)
    sibling = a + 1 - 2 * core
    half = rows // 2
    blocks = rows // 128
    attn_peers = [lax.rem(a + step, 8) for step in range(1, 8)]
    ffn_peers = [lax.rem(f + step, 8) for step in range(1, 8)]
    tp_peers = [lax.rem(t + step, 4) for step in range(1, 4)]

    picked = jnp.dot(r.compact[...], r.h[...], preferred_element_type=F32)
    slot = buf.at[a, t]
    slot[pl.ds(0, rows), :] = (picked * gain[...]).astype(BF)
    squares = picked * picked
    tail = jnp.zeros((16, 128), F32)
    line_index = iota((16, 128), 0)
    for i in range(blocks):
        block = jnp.sum(squares[i * 128 : (i + 1) * 128].T, axis=0, keepdims=True)
        high = block.astype(BF).astype(F32)
        tail = jnp.where(line_index == i, high, tail)
        tail = jnp.where(line_index == blocks + i, block - high, tail)
    slot[pl.ds(rows, 16), :] = tail.astype(BF)

    all_here()

    first = [True]

    def consume(chunk):
        if first[0]:
            loads[0].wait()
            loads[1].wait()
        for c in range(2):
            index = chunk * 2 + c
            depth = pl.ds(pl.multiple_of(index * 512, 512), 512)
            for m in range(0, rows, 256):
                span = pl.ds(m, 256)
                lhs = jnp.concatenate([buf[index, other, span, :] for other in range(4)], axis=1)
                for weight, total in ((wg, gate), (wu, up)):
                    value = lax.dot_general(
                        lhs, weight[:, depth], (((1,), (1,)), ((), ())), preferred_element_type=F32
                    )
                    if first[0] and c == 0:
                        total[span, :] = value
                    else:
                        total[span, :] += value
        first[0] = False

    def settle():
        for copy in pending:
            copy.wait_send()
        return []

    gathered = gather_group(buf, half + 16, *r.normed_sems, consume, settle)
    met()
    sent = []

    tails = jnp.sum(buf[:, :, pl.ds(rows, 16), :].astype(F32).reshape(32, 16, 128), axis=0)
    for i in range(blocks):
        span = pl.ds(i * 128, 128)
        total = tails[i : i + 1] + tails[blocks + i : blocks + i + 1]
        inverse = lax.rsqrt(total / 4096.0 + EPSILON)
        scale = jnp.broadcast_to(inverse, (128, 128)).T
        scale = jnp.concatenate([scale] * 4, axis=1)[:, :448]
        g = gate[span, :] * scale
        act[span, :] = (g / (1.0 + jnp.exp(-g)) * (up[span, :] * scale)).astype(BF)
    loads[2].wait()

    def chunk_columns(dz, c):
        index = lax.rem(z + dz, 4) * 2 + c
        return pl.ds(pl.multiple_of(index * 512, 512), 512)

    def down(dz, c, store):
        for m in range(0, rows, 256):
            span = pl.ds(m, 256)
            store(span, jnp.dot(act[span, :], wd[:, chunk_columns(dz, c)], preferred_element_type=F32))

    def give(i):
        def store(span, value):
            csend[i, span, :] = value.astype(BF)

        down(RS_ORDER[i], 1 - core, store)

    def keep(i):
        def store(span, value):
            part[i, span, :] = value

        down(RS_ORDER[i], core, store)

    def settle_gather():
        for copy in gathered:
            copy.wait_send()

    total, scattered = scatter_group(give, keep, r, settle_gather)
    sums_out[...] = jnp.sum(total, axis=0, keepdims=True)
    spread = jnp.dot(unplace[...], total.astype(BF), preferred_element_type=F32).astype(BF)
    rsend[...] = spread.reshape(8, 4, 16, HD)
    finish()

    def start(copy):
        copy.start()
        sent.append(copy)

    for dz in (2, 1, 3, 0):
        for step in range(8):
            if dz or step:
                to_z, to_f = lax.rem(z + dz, 4), lax.rem(f + step, 8)
                src, dst = rsend.at[to_f, to_z], rbuf.at[z, f]
                start(remote(src, dst, kbs.at[dz, step], kbr.at[dz, step], (to_z * 2 + core, to_f, t)))
    rbuf[z, f] = rsend[f, z]
    for copy in scattered:
        copy.wait_send()
    placing = back[...]
    live_rows = jnp.sum(placing.astype(F32), axis=1, keepdims=True) > 0.5

    def last_copy(dz, from_z, cross, step):
        index = from_z * 2 + core
        src, dst = line.at[from_z, 1 - core if cross else core], final.at[t, index]
        device = (sibling if cross else a, f, lax.rem(t + step, 4))
        return remote(src, dst, kys.at[dz, cross, step], kyr.at[dz, cross, step], device)

    for dz in (0, 1, 3, 2):
        from_z = lax.rem(z + 4 - dz, 4)
        for step in range(8):
            if dz or step:
                slot = rbuf.at[from_z, lax.rem(f + 8 - step, 8)]
                remote(slot, slot, kbs.at[dz, step], kbr.at[dz, step], (sibling, f, t)).wait_recv()
        value = jnp.dot(placing, rbuf[from_z].reshape(128, HD), preferred_element_type=F32)
        value = value + hidden[pl.ds(pl.multiple_of(from_z * 64, 64), 64), :]
        line[from_z] = jnp.where(live_rows, value, 0.0).astype(BF).reshape(2, 32, HD)
        for step in (2, 1, 3):
            start(last_copy(dz, from_z, 0, step))
            start(last_copy(dz, from_z, 1, step))
        start(last_copy(dz, from_z, 1, 0))
        final[t, from_z * 2 + core] = line[from_z, core]
    for dz in (0, 1, 3, 2):
        from_z = lax.rem(z + 4 - dz, 4)
        for cross in range(2):
            for step in range(4):
                if cross or step:
                    slot = final.at[lax.rem(t + 4 - step, 4), from_z * 2 + (1 - core if cross else core)]
                    remote(slot, slot, kys.at[dz, cross, step], kyr.at[dz, cross, step], (sibling, f, t)).wait_recv()
    for other in range(4):
        for source in range(8):
            stream_out[:, pl.ds((source * 4 + other) * HD, HD)] = final[other, source]
    for copy in sent:
        copy.wait_send()


VMEM = pl.BlockSpec(memory_space=pltpu.VMEM)
ANY = pl.BlockSpec(memory_space=pl.ANY)
DMA = pltpu.SemaphoreType.DMA
COMMON = 256

PROJECT_SCRATCH = [
    ("q", pltpu.VMEM((32, 1024), BF)),
    ("k", pltpu.VMEM((32, 128, HD), BF)),
    ("v", pltpu.VMEM((32, 128, HD), BF)),
    ("wout", pltpu.VMEM((4096, HD), BF)),
    ("lens", pltpu.VMEM((1, 32), jnp.int32)),
    ("routes", pltpu.VMEM((1, 32), jnp.int32)),
    ("wide", pltpu.VMEM((8, 128), F32)),
    ("codes", pltpu.VMEM((1, 256), F32)),
    ("heads", pltpu.VMEM((8, 4, 32, 1024), BF)),
    ("res", pltpu.VMEM((8, 32, HD), BF)),
    ("cbuf", pltpu.VMEM((8, 1, 256), F32)),
    ("place", pltpu.VMEM((4, 128, 64), BF)),
    ("sbuf", pltpu.VMEM((4, 8, 16, HD), BF)),
    ("hbuf", pltpu.VMEM((8, 4, 16, HD), BF)),
    ("tsend", pltpu.VMEM((1, 128), F32)),
    ("tbuf", pltpu.VMEM((8, 1, 128), F32)),
    ("in_sems", DMA((6,))),
    *[(name, DMA((7,))) for name in ("rs", "rr", "es", "er", "gs", "gr")],
    ("fs", DMA((4, 7))),
    ("fr", DMA((4, 7))),
    ("own_sem", DMA(())),
    ("targets", pltpu.VMEM((256, 128), jnp.int32)),
    ("hsend", pltpu.VMEM((4, 64, HD), F32)),
    ("hall", pltpu.VMEM((4, 64, HD), F32)),
    ("vs", DMA((4,))),
    ("vr", DMA((4,))),
]


def ffn_scratch(rows):
    return [
        ("wg", pltpu.VMEM((448, 4096), BF)),
        ("wu", pltpu.VMEM((448, 4096), BF)),
        ("wd", pltpu.VMEM((448, 4096), BF)),
        ("compact", pltpu.VMEM((rows, 512), BF)),
        ("buf", pltpu.VMEM((8, 4, rows + 16, HD), BF)),
        ("gate", pltpu.VMEM((rows, 448), F32)),
        ("up", pltpu.VMEM((rows, 448), F32)),
        ("act", pltpu.VMEM((rows, 448), BF)),
        ("csend", pltpu.VMEM((4, rows, 512), BF)),
        ("crecv", pltpu.VMEM((4, rows, 512), BF)),
        ("part", pltpu.VMEM((4, rows, 512), F32)),
        ("y1s", pltpu.VMEM((4, 2, rows, HD), BF)),
        ("y1r", pltpu.VMEM((4, 2, rows, HD), BF)),
        ("y2s", pltpu.VMEM((4, 2, rows // 2, HD), BF)),
        ("y2r", pltpu.VMEM((4, 2, rows // 2, HD), BF)),
        ("zsend", pltpu.VMEM((3, rows, HD), BF)),
        ("zrecv", pltpu.VMEM((3, rows, HD), BF)),
        ("unplace", pltpu.VMEM((512, rows), BF)),
        ("rsend", pltpu.VMEM((8, 4, 16, HD), BF)),
        ("rbuf", pltpu.VMEM((4, 8, 16, HD), BF)),
        ("final", pltpu.VMEM((4, 8, 32, HD), BF)),
        ("line", pltpu.VMEM((4, 2, 32, HD), BF)),
        ("weight_sems", DMA((3,))),
        ("kcs", DMA((4,))),
        ("kcr", DMA((4,))),
        *[(name, DMA((4, 2, 2))) for name in ("k1s", "k1r")],
        *[(name, DMA((4, 2))) for name in ("k2s", "k2r")],
        *[(name, DMA((3, 2))) for name in ("kzs", "kzr")],
        *[(name, DMA((4, 8))) for name in ("kbs", "kbr")],
        *[(name, DMA((4, 2, 4))) for name in ("kys", "kyr")],
    ]


def peers_of():
    a, f, t = position()
    return (
        [(lax.rem(a + step, 8), f, t) for step in range(1, 8)]
        + [(a, lax.rem(f + step, 8), t) for step in range(1, 8)]
        + [(a, f, lax.rem(t + step, 4)) for step in range(1, 4)]
    )


def call(body, name, identity, inputs, outputs, scratch, gathers, operands):
    names = [n for n, _ in inputs] + [n for n, _, _ in outputs] + [n for n, _ in scratch]
    count = len(GATHER_SEMS)

    def kernel(*refs):
        r = types.SimpleNamespace(**dict(zip(names, refs)))
        for i, gather in enumerate(gathers):
            start = len(names) + i * count
            setattr(r, gather, refs[start : start + count])
        body(r)

    return pl.pallas_call(
        kernel,
        name=name,
        out_shape=tuple(shape for _, shape, _ in outputs),
        in_specs=[spec for _, spec in inputs],
        out_specs=[spec for _, _, spec in outputs],
        scratch_shapes=[spec for _, spec in scratch] + GATHER_SEMS * len(gathers),
        compiler_params=pltpu.CompilerParams(
            collective_id=identity, has_side_effects=True, vmem_limit_bytes=63 * 2**20
        ),
    )(*operands)


RESULTS = [
    ("stream", jax.ShapeDtypeStruct((32, 4096), BF), VMEM),
    ("sums", jax.ShapeDtypeStruct((1, HD), F32), VMEM),
]
ROUTED = [
    ("h", jax.ShapeDtypeStruct((512, HD), BF), VMEM),
    ("hidden", jax.ShapeDtypeStruct((256, HD), F32), VMEM),
    ("back", jax.ShapeDtypeStruct((64, 128), BF), VMEM),
    ("table", jax.ShapeDtypeStruct((8, 128), F32), VMEM),
]
WEIGHTS = [("gain", VMEM), ("wg_hbm", ANY), ("wu_hbm", ANY), ("wd_hbm", ANY)]


def layer(*operands):
    def body(r):
        peers = peers_of()
        loads = start_weights(r)
        pending, finish = project_part(r, peers)
        ffn_part(COMMON, r, loads, pending, lambda: None, lambda: None, finish)

    inputs = [
        (name, ANY)
        for name in ("q_hbm", "k_hbm", "v_hbm", "len_hbm", "route_hbm", "res_hbm", "wout_hbm")
    ] + WEIGHTS
    outputs = RESULTS + ROUTED + [
        ("small", jax.ShapeDtypeStruct((1, 1), jnp.int32), pl.BlockSpec(memory_space=pltpu.SMEM))
    ]
    scratch = PROJECT_SCRATCH + ffn_scratch(COMMON)
    return call(body, "layer", 0, inputs, outputs, scratch, ["heads_sems", "normed_sems"], operands)


def feed_forward(rows, identity, *operands):
    def body(r):
        all_here = greet(peers_of())
        loads = start_weights(r)
        positions(rows, r)
        a, f, t = position()

        def meet():
            for step in range(1, 8):
                peer = (a, lax.rem(f + step, 8), t)
                pl.semaphore_signal(r.met, inc=1, device_id=peer, device_id_type=MESH)

        ffn_part(rows, r, loads, [], all_here, meet, lambda: pl.semaphore_wait(r.met, 7))

    inputs = [(name, VMEM) for name, _, _ in ROUTED] + WEIGHTS
    scratch = ffn_scratch(rows) + [("met", pltpu.SemaphoreType.REGULAR)]
    return call(body, "feed_forward", identity, inputs, RESULTS, scratch, ["normed_sems"], operands)


def per_device(
    queries, keys, values, lengths, routes, residual, w_out, norm_gain, w_gate, w_up, w_down
):
    weights = (norm_gain[None, :], w_gate[0].T, w_up[0].T, w_down[0])
    stream, sums, h, hidden, back, table, small = layer(
        queries, keys, values, lengths.reshape(1, 32), routes.reshape(1, 32), residual, w_out, *weights
    )
    return lax.cond(
        small[0, 0] == 1,
        lambda *operands: (stream, sums),
        functools.partial(feed_forward, 512, 1),
        h, hidden, back, table, *weights,
    )


def solution(mesh):
    placed = (
        P(("attn", "ffn"), "tp"),
        P(("attn", "ffn"), None, "tp"),
        P(("attn", "ffn"), None, "tp"),
        P(("attn", "ffn")),
        P(("attn", "ffn"), None),
        P(("attn", "ffn"), None),
        P(None, ("attn", "tp")),
        P(("attn", "tp")),
        P("ffn", None, ("attn", "tp")),
        P("ffn", None, ("attn", "tp")),
        P("ffn", ("attn", "tp"), None),
    )
    return jax.shard_map(
        per_device,
        mesh=mesh,
        in_specs=placed,
        out_specs=(P(("attn", "ffn"), None), P("ffn", ("attn", "tp"))),
        check_vma=False,
    )
```

```python
import functools
import math
import types

import jax
import jax.numpy as jnp
from jax import lax
from jax.experimental import pallas as pl
from jax.experimental.pallas import tpu as pltpu
from jax.sharding import PartitionSpec as P

HD = 128
EPSILON = 1e-05
MESH = pl.DeviceIdType.MESH
BF = jnp.bfloat16
F32 = jnp.float32
Z_ORDER = (1, 3, 2)
RS_ORDER = (2, 1, 3, 0)


def upper_half(rows):
    return (rows // 16 + 1) // 2 * 16


def iota(shape, dim):
    return lax.broadcasted_iota(jnp.int32, shape, dim)


def position():
    return lax.axis_index("attn"), lax.axis_index("ffn"), lax.axis_index("tp")


def remote(src, dst, send, recv, device):
    return pltpu.make_async_remote_copy(
        src_ref=src, dst_ref=dst, send_sem=send, recv_sem=recv, device_id=device, device_id_type=MESH
    )


def greet(devices):
    barrier = pltpu.get_barrier_semaphore()
    for device in devices:
        pl.semaphore_signal(barrier, inc=1, device_id=device, device_id_type=MESH)
    return lambda: pl.semaphore_wait(barrier, len(devices))


def gather_group(buf, half, zs, zr, ys, yr, hs, hr, cs, cr, consume, meanwhile=None):
    a, f, t = position()
    right, left = lax.rem(t + 1, 4), lax.rem(t + 3, 4)
    opposite = lax.rem(t + 2, 4)
    sibling = a + 1 - 2 * lax.rem(a, 2)
    rows = buf.shape[2]
    pieces = (pl.ds(0, half), pl.ds(half, rows - half))
    source = [a] + [lax.rem(a + 8 - 2 * dz, 8) for dz in Z_ORDER]
    sent = []

    def start(copy):
        copy.start()
        sent.append(copy)

    def z_send(k, h):
        piece = buf.at[a, t].at[pieces[h]]
        start(remote(piece, piece, zs.at[k, h], zr.at[k, h], (lax.rem(a + 2 * Z_ORDER[k], 8), f, t)))

    def z_wait(k, h):
        piece = buf.at[source[k + 1], t].at[pieces[h]]
        remote(piece, piece, zs.at[k, h], zr.at[k, h], (a, f, right)).wait_recv()

    def z_forward(h):
        piece = buf.at[source[2 if h else 1], t].at[pieces[h]]
        z = lax.rem(a + (6 if h else 2), 8)
        start(remote(piece, piece, zs.at[2, h], zr.at[2, h], (z, f, t)))

    def y_copy(k, slot, h, way):
        piece = buf.at[source[k], slot].at[pieces[h]]
        return remote(piece, piece, ys.at[k, way, h], yr.at[k, way, h], (a, f, left if way else right))

    def y_send(k, h):
        start(y_copy(k, t, h, h))
        start(y_copy(k, t, h, 1 - h))
        if k == 3:
            piece = buf.at[source[k], t].at[pieces[h]]
            start(remote(piece, piece, hs.at[k, h], hr.at[k, h], (a, f, opposite)))

    def y_forward(k):
        if k == 3:
            return
        for h in range(2):
            slot = right if h else left
            y_copy(k, slot, h, h).wait_recv()
            piece = buf.at[source[k], slot].at[pieces[h]]
            start(remote(piece, piece, hs.at[k, h], hr.at[k, h], (a, f, left if h else right)))

    def core_send(k):
        if k == 3:
            for h in range(2):
                y_copy(k, right if h else left, h, h).wait_recv()
        for h in range(2):
            y_copy(k, left if h else right, h, 1 - h).wait_recv()
        for h in range(2):
            piece = buf.at[source[k], opposite].at[pieces[h]]
            remote(piece, piece, hs.at[k, h], hr.at[k, h], (a, f, right)).wait_recv()
        chunk = buf.at[source[k]]
        start(remote(chunk, chunk, cs.at[k], cr.at[k], (sibling, f, t)))

    def core_wait(k):
        other = source[k] + 1 - 2 * lax.rem(a, 2)
        chunk = buf.at[other]
        remote(chunk, chunk, cs.at[k], cr.at[k], (sibling, f, t)).wait_recv()
        consume(lax.div(source[k], 2))

    z_send(0, 0)
    z_send(1, 1)
    z_send(0, 1)
    z_send(1, 0)
    y_send(0, 0)
    y_send(0, 1)
    if meanwhile is not None:
        sent.extend(meanwhile())
    z_wait(0, 0)
    z_forward(0)
    y_send(1, 0)
    z_wait(1, 1)
    z_forward(1)
    y_send(2, 1)
    z_wait(0, 1)
    y_send(1, 1)
    z_wait(1, 0)
    y_send(2, 0)
    y_forward(0)
    for h in range(2):
        z_wait(2, h)
        y_send(3, h)
    y_forward(1)
    y_forward(2)
    core_send(0)
    core_send(1)
    core_wait(0)
    y_forward(3)
    core_send(2)
    core_wait(1)
    core_send(3)
    core_wait(2)
    core_wait(3)
    return sent


GATHER_SEMS = [
    pltpu.SemaphoreType.DMA((3, 2)),
    pltpu.SemaphoreType.DMA((3, 2)),
    pltpu.SemaphoreType.DMA((4, 2, 2)),
    pltpu.SemaphoreType.DMA((4, 2, 2)),
    pltpu.SemaphoreType.DMA((4, 2)),
    pltpu.SemaphoreType.DMA((4, 2)),
    pltpu.SemaphoreType.DMA((4,)),
    pltpu.SemaphoreType.DMA((4,)),
]


def scatter_group(give, keep, r, settle):
    a, f, t = position()
    right, left, opposite = lax.rem(t + 1, 4), lax.rem(t + 3, 4), lax.rem(t + 2, 4)
    sibling = a + 1 - 2 * lax.rem(a, 2)
    csend, crecv, part, y1s, y1r, y2s, y2r, zsend, zrecv = (
        r.csend, r.crecv, r.part, r.y1s, r.y1r, r.y2s, r.y2r, r.zsend, r.zrecv
    )
    half = upper_half(part.shape[1])
    sizes = (half, part.shape[1] - half)
    halves = (pl.ds(0, sizes[0]), pl.ds(half, sizes[1]))
    starts = (pl.ds(0, sizes[0]), pl.ds(0, sizes[1]))
    sent = []

    def start(copy):
        copy.start()
        sent.append(copy)

    def block(i, span, index):
        lanes = pl.ds(pl.multiple_of(index * HD, HD), HD)
        return part[i, span, lanes] + crecv[i, span, lanes].astype(F32)

    def core_copy(i):
        return remote(csend.at[i], crecv.at[i], r.kcs.at[i], r.kcr.at[i], (sibling, f, t))

    def first_copy(i, way, h):
        src, dst = y1s.at[i, way, halves[h]], y1r.at[i, way, halves[h]]
        return remote(src, dst, r.k1s.at[i, way, h], r.k1r.at[i, way, h], (a, f, left if way else right))

    def second_copy(i, way):
        device = (a, f, left if way else right)
        src, dst = y2s.at[i, way, starts[way]], y2r.at[i, way, starts[way]]
        return remote(src, dst, r.k2s.at[i, way], r.k2r.at[i, way], device)

    def z_copy(i, h):
        src, dst = zsend.at[i, halves[h]], zrecv.at[i, halves[h]]
        return remote(src, dst, r.kzs.at[i, h], r.kzr.at[i, h], (lax.rem(a + 2 * RS_ORDER[i], 8), f, t))

    def core_give(i):
        give(i)
        start(core_copy(i))
        keep(i)

    def y_first(i):
        core_copy(i).wait_recv()
        for way in range(2):
            y1s[i, way, halves[way], :] = block(i, halves[way], opposite).astype(BF)
            start(first_copy(i, way, way))
        for way in range(2):
            span = halves[1 - way]
            y1s[i, way, span, :] = block(i, span, left if way else right).astype(BF)
            start(first_copy(i, way, 1 - way))

    def y_second(i):
        for way in range(2):
            value = block(i, halves[way], left if way else right)
            first_copy(i, way, way).wait_recv()
            y2s[i, way, starts[way], :] = (value + y1r[i, way, halves[way], :].astype(F32)).astype(BF)
            start(second_copy(i, way))

    def y_sum(i, h):
        value = block(i, halves[h], t)
        first_copy(i, 1 - h, h).wait_recv()
        value = value + y1r[i, 1 - h, halves[h], :].astype(F32)
        second_copy(i, h).wait_recv()
        return value + y2r[i, h, starts[h], :].astype(F32)

    def z_give(i):
        for h in range(2):
            zsend[i, halves[h], :] = y_sum(i, h).astype(BF)
            start(z_copy(i, h))

    core_give(0)
    core_give(1)
    y_first(0)
    core_give(2)
    y_first(1)
    y_second(0)
    core_give(3)
    y_first(2)
    y_second(1)
    y_first(3)
    settle()
    z_give(0)
    y_second(2)
    z_give(1)
    y_second(3)
    z_give(2)
    total = []
    for h in range(2):
        value = y_sum(3, h)
        for i in range(3):
            z_copy(i, h).wait_recv()
            value = value + zrecv[i, halves[h], :].astype(F32)
        total.append(value)
    return jnp.concatenate(total, axis=0), sent


def attend(q, k, v, lens, att):
    for part in range(2):
        base = part * 16
        heads = jnp.concatenate([q[base : base + 16, h * HD : (h + 1) * HD] for h in range(8)], axis=0)
        slot = lax.rem(iota((128, 128), 0), 16)
        scores = jnp.zeros((128, 128), F32)
        for pair in range(8):
            block = k[base + 2 * pair : base + 2 * pair + 2].reshape(256, HD)
            both = lax.dot_general(heads, block, (((1,), (1,)), ((), ())), preferred_element_type=F32)
            scores = jnp.where(slot == 2 * pair, both[:, :128], scores)
            scores = jnp.where(slot == 2 * pair + 1, both[:, 128:], scores)
        scores = scores / math.sqrt(HD)
        limit = jnp.concatenate([lens[base : base + 16, :]] * 8, axis=0)
        valid = iota((128, 128), 1) < limit
        top = jnp.max(jnp.where(valid, scores, -1e30), axis=-1, keepdims=True)
        unnormed = jnp.where(valid, jnp.exp(scores - top), 0.0)
        summed = jnp.maximum(jnp.sum(unnormed, axis=-1, keepdims=True), 1.0)
        weights = unnormed / summed
        total = jnp.zeros((128, HD), F32)
        for pair in range(8):
            block = v[base + 2 * pair : base + 2 * pair + 2].reshape(256, HD)
            masked = jnp.concatenate(
                [jnp.where(slot == 2 * pair, weights, 0.0), jnp.where(slot == 2 * pair + 1, weights, 0.0)], axis=1
            ).astype(BF)
            total = total + jnp.dot(masked, block, preferred_element_type=F32)
        total = total.astype(BF)
        for h in range(8):
            att[pl.ds(base, 16), pl.ds(h * HD, HD)] = total[h * 16 : (h + 1) * 16, :]


def project_part(r, peers):
    a, f, t = position()
    q, k, v, wout, lens, routes, wide, codes, buf, res = (
        r.q, r.k, r.v, r.wout, r.lens, r.routes, r.wide, r.codes, r.heads, r.res
    )
    cbuf, place, sbuf, hbuf, tsend, tbuf = r.cbuf, r.place, r.sbuf, r.hbuf, r.tsend, r.tbuf
    in_sems, rs, rr, es, er, fs, fr, gs, gr = r.in_sems, r.rs, r.rr, r.es, r.er, r.fs, r.fr, r.gs, r.gr
    back_out, res_hbm, hsend, hall = r.back, r.res_hbm, r.hsend, r.hall
    own_z, core = lax.div(a, 2), lax.rem(a, 2)
    attn_peers = [lax.rem(a + step, 8) for step in range(1, 8)]
    ffn_peers = [lax.rem(f + step, 8) for step in range(1, 8)]
    all_here = greet(peers)
    loads = []
    pairs = (
        (r.len_hbm, lens), (r.route_hbm, routes), (r.q_hbm, q), (r.k_hbm, k), (r.v_hbm, v), (r.wout_hbm, wout),
    )
    for i, (src, dst) in enumerate(pairs):
        copy = pltpu.make_async_copy(src, dst, in_sems.at[i])
        copy.start()
        loads.append(copy)

    def columns(index):
        return pl.ds(pl.multiple_of((index * 4 + t) * HD, HD), HD)

    loads[0].wait()
    loads[1].wait()
    wide[...] = jnp.zeros((8, 128), F32)
    wide[0:1, 0:32] = lens[...].astype(F32)
    wide[1:2, 0:32] = jnp.where(lens[...] > 0, routes[...], 8).astype(F32) + 1.0
    limits = jnp.broadcast_to(wide[0:1, :], (128, 128)).T[:32].astype(jnp.int32)
    tile = jnp.where(iota((128, 256), 0) == lax.rem(iota((128, 256), 1), 32), 1.0, 0.0).astype(BF)
    tiled = jnp.dot(jnp.broadcast_to(wide[1:2, :], (16, 128)).astype(BF), tile, preferred_element_type=F32)
    codes[...] = jnp.where(iota((1, 256), 1) // 32 == a, tiled[:1], 0.0)
    for copy in loads[2:5]:
        copy.wait()
    attend(q, k, v, limits, buf.at[a, t])
    cbuf[a] = codes[...]
    own = pltpu.make_async_copy(res_hbm.at[:, columns(a)], res.at[a], r.own_sem)
    own.start()
    all_here()

    def exchange():
        sent = []
        for i, peer in enumerate(attn_peers):
            copy = remote(codes, cbuf.at[a], es.at[i], er.at[i], (peer, f, t))
            copy.start()
            sent.append(copy)
            copy = remote(res_hbm.at[:, columns(peer)], res.at[a], rs.at[i], rr.at[i], (peer, f, t))
            copy.start()
            sent.append(copy)
        return sent

    def prepare():
        loads[5].wait()
        own.wait()
        for i in range(7):
            peer = lax.rem(a + 7 - i, 8)
            remote(cbuf.at[peer], cbuf.at[peer], es.at[i], er.at[i], (peer, f, t)).wait_recv()
        code = cbuf[0]
        for i in range(1, 8):
            code = code + cbuf[i]
        code = code - 1.0
        code_t = jnp.broadcast_to(code, (256, 256)).T
        down, across = iota((256, 256), 0), iota((256, 256), 1)
        same = (code_t == code) & (down // 32 == across // 32)
        rank_row = jnp.sum(jnp.where(same & (down < across), 1.0, 0.0), axis=0, keepdims=True)
        rank_col = jnp.sum(jnp.where(same & (across < down), 1.0, 0.0), axis=1, keepdims=True)
        target_row = (code * 8.0 + rank_row).astype(jnp.int32)
        target_col = (code_t[:, 0:1] * 8.0 + rank_col).astype(jnp.int32)
        p, q_index = iota((512, 64), 0), iota((512, 64), 1)
        wanted = (lax.rem(p, 128) // 16) * 8 + lax.rem(p, 8)
        of_z = jnp.concatenate(
            [jnp.broadcast_to(target_row[:, z * 64 : (z + 1) * 64], (128, 64)) for z in range(4)], axis=0
        )
        hit = (wanted == of_z) & (lax.rem(p // 8, 2) == q_index // 32)
        place[...] = jnp.where(hit, 1.0, 0.0).astype(BF).reshape(4, 128, 64)
        r.targets[...] = jnp.broadcast_to(target_col, (256, 128))
        own_targets = r.targets[pl.ds(pl.multiple_of(own_z * 64, 64), 64), :]
        q_index, p = iota((64, 128), 0), iota((64, 128), 1)
        hit = ((p // 16) * 8 + lax.rem(p, 8) == own_targets) & (lax.rem(p // 8, 2) == q_index // 32)
        back_out[...] = jnp.where(hit, 1.0, 0.0).astype(BF)
        q_index, j = iota((256, 128), 0), iota((256, 128), 1)
        block = (q_index // 32 == lax.rem(j, 8)) & (j < 64)
        named = (code_t[:, :128] == (j // 8).astype(F32)) & block
        tsend[...] = jnp.sum(jnp.where(named, 1.0, 0.0), axis=0, keepdims=True)
        tbuf[f] = tsend[...]
        for i in range(7):
            peer = lax.rem(a + 7 - i, 8)
            remote(res.at[peer], res.at[peer], rs.at[i], rr.at[i], (peer, f, t)).wait_recv()

    later = []
    chunks = []

    def consume(z):
        if not chunks:
            prepare()
            for i, peer in enumerate(ffn_peers):
                copy = remote(tsend, tbuf.at[f], gs.at[i], gr.at[i], (a, peer, t))
                copy.start()
                later.append(copy)
        number = len(chunks)
        chunks.append(z)
        pair = pl.ds(2 * z, 2)
        total = jnp.zeros((64, HD), F32)
        for other in range(4):
            left = buf[pair, other].reshape(64, 1024)
            total = total + jnp.dot(left, wout[pl.ds(other * 1024, 1024), :], preferred_element_type=F32)
        total = total + res[pair].reshape(64, HD).astype(F32)
        if number:
            hsend[z] = total
        else:
            hall[z] = total
        routed = jnp.dot(place[z], total.astype(BF), preferred_element_type=F32).astype(BF)
        sbuf[z] = routed.reshape(8, 16, HD)
        for i, peer in enumerate(ffn_peers):
            copy = remote(sbuf.at[z, peer], hbuf.at[f, z], fs.at[number, i], fr.at[number, i], (a, peer, t))
            copy.start()
            later.append(copy)
        hbuf[f, z] = sbuf[z, f]
        if number:
            copy = remote(hsend.at[z], hall.at[own_z], r.vs.at[number], r.vr.at[number], (z * 2 + core, f, t))
            copy.start()
            later.append(copy)

    sent = gather_group(buf, 16, *r.heads_sems, consume, exchange)
    for i in range(7):
        peer = lax.rem(f + 7 - i, 8)
        remote(tbuf.at[peer], tbuf.at[peer], gs.at[i], gr.at[i], (a, peer, t)).wait_recv()
    table = tbuf[...].reshape(8, 128)
    r.table[...] = table
    sums = jnp.broadcast_to(jnp.sum(table, axis=0, keepdims=True), (16, 128)).astype(BF)
    fold = jnp.where(iota((128, 128), 0) // 8 == iota((128, 128), 1), 1.0, 0.0).astype(BF)
    totals = jnp.dot(sums, fold, preferred_element_type=F32)
    r.small[0, 0] = jnp.where(jnp.max(totals) <= float(COMMON), 1, 0)
    positions(COMMON, r)
    for number, z in enumerate(chunks):
        for i in range(7):
            peer = lax.rem(f + 7 - i, 8)
            slot = hbuf.at[peer, z]
            remote(slot, slot, fs.at[number, i], fr.at[number, i], (a, peer, t)).wait_recv()
    r.h[...] = hbuf[...].reshape(512, HD)

    def finish():
        for i, dz in enumerate(Z_ORDER):
            slot = hall.at[lax.rem(own_z + dz, 4)]
            remote(slot, slot, r.vs.at[i + 1], r.vr.at[i + 1], (lax.rem(a + 2 * dz, 8), f, t)).wait_recv()
        r.hidden[...] = hall[...].reshape(256, HD)

    return sent + later, finish


def start_weights(r):
    loads = []
    for i, (src, dst) in enumerate(((r.wg_hbm, r.wg), (r.wu_hbm, r.wu), (r.wd_hbm, r.wd))):
        copy = pltpu.make_async_copy(src, dst, r.weight_sems.at[i])
        copy.start()
        loads.append(copy)
    return loads


def positions(rows, r):
    f = lax.axis_index("ffn")
    j, p = iota((128, 512), 0), iota((128, 512), 1)
    pick = jnp.where(j == f * 8 + lax.rem(p // 8, 8), 1.0, 0.0).astype(BF)
    table16 = jnp.concatenate([r.table[...], r.table[...]], axis=0).astype(BF)
    counts = jnp.dot(table16, pick, preferred_element_type=F32)[:8]
    s, p = iota((8, 512), 0), iota((8, 512), 1)
    counts = jnp.sum(jnp.where(s == p // 64, counts, 0.0), axis=0, keepdims=True)
    live = lax.rem(iota((1, 512), 1), 8).astype(F32) < counts
    flags = jnp.broadcast_to(jnp.where(live, 1.0, 0.0), (16, 512)).astype(BF)
    before = jnp.where(iota((512, 512), 0) < iota((512, 512), 1), 1.0, 0.0).astype(BF)
    place = jnp.dot(flags, before, preferred_element_type=F32)[:1]
    place = jnp.where(live, place, -1.0)
    r.compact[...] = jnp.where(iota((rows, 512), 0) == place.astype(jnp.int32), 1.0, 0.0).astype(BF)
    place_t = jnp.broadcast_to(place, (128, 512)).T.astype(jnp.int32)
    for i in range(-(-rows // 128)):
        hit = place_t == iota((512, 128), 1) + i * 128
        r.unplace[:, pl.ds(i * 128, 128)] = jnp.where(hit, 1.0, 0.0).astype(BF)


def ffn_part(rows, r, loads, pending, all_here, met, finish):
    a, f, t = position()
    hidden, back, gain, stream_out, sums_out = r.hidden, r.back, r.gain, r.stream, r.sums
    wg, wu, wd, buf, gate, up, act = r.wg, r.wu, r.wd, r.buf, r.gate, r.up, r.act
    csend, part, unplace, rsend, rbuf, final, line = r.csend, r.part, r.unplace, r.rsend, r.rbuf, r.final, r.line
    kbs, kbr, kys, kyr = r.kbs, r.kbr, r.kys, r.kyr
    z, core = lax.div(a, 2), lax.rem(a, 2)
    right, left, opposite = lax.rem(t + 1, 4), lax.rem(t + 3, 4), lax.rem(t + 2, 4)
    sibling = a + 1 - 2 * core
    blocks = -(-rows // 128)
    padding = jnp.zeros((blocks * 128 - rows, HD), F32)
    tiles = [pl.ds(0, rows)] if rows < 384 else [pl.ds(m, 256) for m in range(0, rows, 256)]

    def padded(value):
        return jnp.concatenate([value, padding], axis=0) if blocks * 128 > rows else value

    attn_peers = [lax.rem(a + step, 8) for step in range(1, 8)]
    ffn_peers = [lax.rem(f + step, 8) for step in range(1, 8)]
    tp_peers = [lax.rem(t + step, 4) for step in range(1, 4)]

    picked = jnp.dot(r.compact[...], r.h[...], preferred_element_type=F32)
    slot = buf.at[a, t]
    slot[pl.ds(0, rows), :] = (picked * gain[...]).astype(BF)
    squares = padded(picked * picked)
    tail = jnp.zeros((16, 128), F32)
    line_index = iota((16, 128), 0)
    for i in range(blocks):
        block = jnp.sum(squares[i * 128 : (i + 1) * 128].T, axis=0, keepdims=True)
        high = block.astype(BF).astype(F32)
        tail = jnp.where(line_index == i, high, tail)
        tail = jnp.where(line_index == blocks + i, block - high, tail)
    slot[pl.ds(rows, 16), :] = tail.astype(BF)

    all_here()

    first = [True]

    def consume(chunk):
        if first[0]:
            loads[0].wait()
            loads[1].wait()
        for c in range(2):
            index = chunk * 2 + c
            depth = pl.ds(pl.multiple_of(index * 512, 512), 512)
            for span in tiles:
                lhs = jnp.concatenate([buf[index, other, span, :] for other in range(4)], axis=1)
                for weight, total in ((wg, gate), (wu, up)):
                    value = lax.dot_general(
                        lhs, weight[:, depth], (((1,), (1,)), ((), ())), preferred_element_type=F32
                    )
                    if first[0] and c == 0:
                        total[span, :] = value
                    else:
                        total[span, :] += value
        first[0] = False

    def settle():
        for copy in pending:
            copy.wait_send()
        return []

    gathered = gather_group(buf, upper_half(rows + 16), *r.normed_sems, consume, settle)
    met()
    sent = []

    tails = jnp.sum(buf[:, :, pl.ds(rows, 16), :].astype(F32).reshape(32, 16, 128), axis=0)
    for i in range(blocks):
        size = min(128, rows - i * 128)
        span = pl.ds(i * 128, size)
        total = tails[i : i + 1] + tails[blocks + i : blocks + i + 1]
        inverse = lax.rsqrt(total / 4096.0 + EPSILON)
        scale = jnp.broadcast_to(inverse, (128, 128)).T
        scale = jnp.concatenate([scale] * 4, axis=1)[:size, :448]
        g = gate[span, :] * scale
        act[span, :] = (g / (1.0 + jnp.exp(-g)) * (up[span, :] * scale)).astype(BF)
    loads[2].wait()

    def chunk_columns(dz, c):
        index = lax.rem(z + dz, 4) * 2 + c
        return pl.ds(pl.multiple_of(index * 512, 512), 512)

    def down(dz, c, store):
        for span in tiles:
            store(span, jnp.dot(act[span, :], wd[:, chunk_columns(dz, c)], preferred_element_type=F32))

    def give(i):
        def store(span, value):
            csend[i, span, :] = value.astype(BF)

        down(RS_ORDER[i], 1 - core, store)

    def keep(i):
        def store(span, value):
            part[i, span, :] = value

        down(RS_ORDER[i], core, store)

    def settle_gather():
        for copy in gathered:
            copy.wait_send()

    total, scattered = scatter_group(give, keep, r, settle_gather)
    sums_out[...] = jnp.sum(total, axis=0, keepdims=True)
    spread = jnp.dot(unplace[...], padded(total).astype(BF), preferred_element_type=F32).astype(BF)
    rsend[...] = spread.reshape(8, 4, 16, HD)
    finish()

    def start(copy):
        copy.start()
        sent.append(copy)

    for dz in (2, 1, 3, 0):
        for step in range(8):
            if dz or step:
                to_z, to_f = lax.rem(z + dz, 4), lax.rem(f + step, 8)
                src, dst = rsend.at[to_f, to_z], rbuf.at[z, f]
                start(remote(src, dst, kbs.at[dz, step], kbr.at[dz, step], (to_z * 2 + core, to_f, t)))
    rbuf[z, f] = rsend[f, z]
    for copy in scattered:
        copy.wait_send()
    placing = back[...]
    live_rows = jnp.sum(placing.astype(F32), axis=1, keepdims=True) > 0.5

    def last_copy(dz, from_z, cross, step):
        index = from_z * 2 + core
        src, dst = line.at[from_z, 1 - core if cross else core], final.at[t, index]
        device = (sibling if cross else a, f, lax.rem(t + step, 4))
        return remote(src, dst, kys.at[dz, cross, step], kyr.at[dz, cross, step], device)

    for dz in (0, 1, 3, 2):
        from_z = lax.rem(z + 4 - dz, 4)
        for step in range(8):
            if dz or step:
                slot = rbuf.at[from_z, lax.rem(f + 8 - step, 8)]
                remote(slot, slot, kbs.at[dz, step], kbr.at[dz, step], (sibling, f, t)).wait_recv()
        value = jnp.dot(placing, rbuf[from_z].reshape(128, HD), preferred_element_type=F32)
        value = value + hidden[pl.ds(pl.multiple_of(from_z * 64, 64), 64), :]
        line[from_z] = jnp.where(live_rows, value, 0.0).astype(BF).reshape(2, 32, HD)
        for step in (2, 1, 3):
            start(last_copy(dz, from_z, 0, step))
            start(last_copy(dz, from_z, 1, step))
        start(last_copy(dz, from_z, 1, 0))
        final[t, from_z * 2 + core] = line[from_z, core]
    for dz in (0, 1, 3, 2):
        from_z = lax.rem(z + 4 - dz, 4)
        for cross in range(2):
            for step in range(4):
                if cross or step:
                    slot = final.at[lax.rem(t + 4 - step, 4), from_z * 2 + (1 - core if cross else core)]
                    remote(slot, slot, kys.at[dz, cross, step], kyr.at[dz, cross, step], (sibling, f, t)).wait_recv()
    for other in range(4):
        for source in range(8):
            stream_out[:, pl.ds((source * 4 + other) * HD, HD)] = final[other, source]
    for copy in sent:
        copy.wait_send()


VMEM = pl.BlockSpec(memory_space=pltpu.VMEM)
ANY = pl.BlockSpec(memory_space=pl.ANY)
DMA = pltpu.SemaphoreType.DMA
COMMON = 272

PROJECT_SCRATCH = [
    ("q", pltpu.VMEM((32, 1024), BF)),
    ("k", pltpu.VMEM((32, 128, HD), BF)),
    ("v", pltpu.VMEM((32, 128, HD), BF)),
    ("wout", pltpu.VMEM((4096, HD), BF)),
    ("lens", pltpu.VMEM((1, 32), jnp.int32)),
    ("routes", pltpu.VMEM((1, 32), jnp.int32)),
    ("wide", pltpu.VMEM((8, 128), F32)),
    ("codes", pltpu.VMEM((1, 256), F32)),
    ("heads", pltpu.VMEM((8, 4, 32, 1024), BF)),
    ("res", pltpu.VMEM((8, 32, HD), BF)),
    ("cbuf", pltpu.VMEM((8, 1, 256), F32)),
    ("place", pltpu.VMEM((4, 128, 64), BF)),
    ("sbuf", pltpu.VMEM((4, 8, 16, HD), BF)),
    ("hbuf", pltpu.VMEM((8, 4, 16, HD), BF)),
    ("tsend", pltpu.VMEM((1, 128), F32)),
    ("tbuf", pltpu.VMEM((8, 1, 128), F32)),
    ("in_sems", DMA((6,))),
    *[(name, DMA((7,))) for name in ("rs", "rr", "es", "er", "gs", "gr")],
    ("fs", DMA((4, 7))),
    ("fr", DMA((4, 7))),
    ("own_sem", DMA(())),
    ("targets", pltpu.VMEM((256, 128), jnp.int32)),
    ("hsend", pltpu.VMEM((4, 64, HD), F32)),
    ("hall", pltpu.VMEM((4, 64, HD), F32)),
    ("vs", DMA((4,))),
    ("vr", DMA((4,))),
]


def ffn_scratch(rows):
    return [
        ("wg", pltpu.VMEM((448, 4096), BF)),
        ("wu", pltpu.VMEM((448, 4096), BF)),
        ("wd", pltpu.VMEM((448, 4096), BF)),
        ("compact", pltpu.VMEM((rows, 512), BF)),
        ("buf", pltpu.VMEM((8, 4, rows + 16, HD), BF)),
        ("gate", pltpu.VMEM((rows, 448), F32)),
        ("up", pltpu.VMEM((rows, 448), F32)),
        ("act", pltpu.VMEM((rows, 448), BF)),
        ("csend", pltpu.VMEM((4, rows, 512), BF)),
        ("crecv", pltpu.VMEM((4, rows, 512), BF)),
        ("part", pltpu.VMEM((4, rows, 512), F32)),
        ("y1s", pltpu.VMEM((4, 2, rows, HD), BF)),
        ("y1r", pltpu.VMEM((4, 2, rows, HD), BF)),
        ("y2s", pltpu.VMEM((4, 2, upper_half(rows), HD), BF)),
        ("y2r", pltpu.VMEM((4, 2, upper_half(rows), HD), BF)),
        ("zsend", pltpu.VMEM((3, rows, HD), BF)),
        ("zrecv", pltpu.VMEM((3, rows, HD), BF)),
        ("unplace", pltpu.VMEM((512, -(-rows // 128) * 128), BF)),
        ("rsend", pltpu.VMEM((8, 4, 16, HD), BF)),
        ("rbuf", pltpu.VMEM((4, 8, 16, HD), BF)),
        ("final", pltpu.VMEM((4, 8, 32, HD), BF)),
        ("line", pltpu.VMEM((4, 2, 32, HD), BF)),
        ("weight_sems", DMA((3,))),
        ("kcs", DMA((4,))),
        ("kcr", DMA((4,))),
        *[(name, DMA((4, 2, 2))) for name in ("k1s", "k1r")],
        *[(name, DMA((4, 2))) for name in ("k2s", "k2r")],
        *[(name, DMA((3, 2))) for name in ("kzs", "kzr")],
        *[(name, DMA((4, 8))) for name in ("kbs", "kbr")],
        *[(name, DMA((4, 2, 4))) for name in ("kys", "kyr")],
    ]


def peers_of():
    a, f, t = position()
    return (
        [(lax.rem(a + step, 8), f, t) for step in range(1, 8)]
        + [(a, lax.rem(f + step, 8), t) for step in range(1, 8)]
        + [(a, f, lax.rem(t + step, 4)) for step in range(1, 4)]
    )


def call(body, name, identity, inputs, outputs, scratch, gathers, operands):
    names = [n for n, _ in inputs] + [n for n, _, _ in outputs] + [n for n, _ in scratch]
    count = len(GATHER_SEMS)

    def kernel(*refs):
        r = types.SimpleNamespace(**dict(zip(names, refs)))
        for i, gather in enumerate(gathers):
            start = len(names) + i * count
            setattr(r, gather, refs[start : start + count])
        body(r)

    return pl.pallas_call(
        kernel,
        name=name,
        out_shape=tuple(shape for _, shape, _ in outputs),
        in_specs=[spec for _, spec in inputs],
        out_specs=[spec for _, _, spec in outputs],
        scratch_shapes=[spec for _, spec in scratch] + GATHER_SEMS * len(gathers),
        compiler_params=pltpu.CompilerParams(
            collective_id=identity, has_side_effects=True, vmem_limit_bytes=63 * 2**20
        ),
    )(*operands)


RESULTS = [
    ("stream", jax.ShapeDtypeStruct((32, 4096), BF), VMEM),
    ("sums", jax.ShapeDtypeStruct((1, HD), F32), VMEM),
]
ROUTED = [
    ("h", jax.ShapeDtypeStruct((512, HD), BF), VMEM),
    ("hidden", jax.ShapeDtypeStruct((256, HD), F32), VMEM),
    ("back", jax.ShapeDtypeStruct((64, 128), BF), VMEM),
    ("table", jax.ShapeDtypeStruct((8, 128), F32), VMEM),
]
WEIGHTS = [("gain", VMEM), ("wg_hbm", ANY), ("wu_hbm", ANY), ("wd_hbm", ANY)]


def layer(*operands):
    def body(r):
        peers = peers_of()
        loads = start_weights(r)
        pending, finish = project_part(r, peers)
        ffn_part(COMMON, r, loads, pending, lambda: None, lambda: None, finish)

    inputs = [
        (name, ANY)
        for name in ("q_hbm", "k_hbm", "v_hbm", "len_hbm", "route_hbm", "res_hbm", "wout_hbm")
    ] + WEIGHTS
    outputs = RESULTS + ROUTED + [
        ("small", jax.ShapeDtypeStruct((1, 1), jnp.int32), pl.BlockSpec(memory_space=pltpu.SMEM))
    ]
    scratch = PROJECT_SCRATCH + ffn_scratch(COMMON)
    return call(body, "layer", 0, inputs, outputs, scratch, ["heads_sems", "normed_sems"], operands)


def feed_forward(rows, identity, *operands):
    def body(r):
        all_here = greet(peers_of())
        loads = start_weights(r)
        positions(rows, r)
        a, f, t = position()

        def meet():
            for step in range(1, 8):
                peer = (a, lax.rem(f + step, 8), t)
                pl.semaphore_signal(r.met, inc=1, device_id=peer, device_id_type=MESH)

        ffn_part(rows, r, loads, [], all_here, meet, lambda: pl.semaphore_wait(r.met, 7))

    inputs = [(name, VMEM) for name, _, _ in ROUTED] + WEIGHTS
    scratch = ffn_scratch(rows) + [("met", pltpu.SemaphoreType.REGULAR)]
    return call(body, "feed_forward", identity, inputs, RESULTS, scratch, ["normed_sems"], operands)


def per_device(
    queries, keys, values, lengths, routes, residual, w_out, norm_gain, w_gate, w_up, w_down
):
    weights = (norm_gain[None, :], w_gate[0].T, w_up[0].T, w_down[0])
    stream, sums, h, hidden, back, table, small = layer(
        queries, keys, values, lengths.reshape(1, 32), routes.reshape(1, 32), residual, w_out, *weights
    )
    return lax.cond(
        small[0, 0] == 1,
        lambda *operands: (stream, sums),
        functools.partial(feed_forward, 512, 1),
        h, hidden, back, table, *weights,
    )


def solution(mesh):
    placed = (
        P(("attn", "ffn"), "tp"),
        P(("attn", "ffn"), None, "tp"),
        P(("attn", "ffn"), None, "tp"),
        P(("attn", "ffn")),
        P(("attn", "ffn"), None),
        P(("attn", "ffn"), None),
        P(None, ("attn", "tp")),
        P(("attn", "tp")),
        P("ffn", None, ("attn", "tp")),
        P("ffn", None, ("attn", "tp")),
        P("ffn", ("attn", "tp"), None),
    )
    return jax.shard_map(
        per_device,
        mesh=mesh,
        in_specs=placed,
        out_specs=(P(("attn", "ffn"), None), P("ffn", ("attn", "tp"))),
        check_vma=False,
    )
```
